256 devices in a mesh: ctx: 32 (over x, z), expert: 8 (over y, core).
Axes of the slice: x: 4, y: 4, z: 8, core: 2. Of those that a mesh axis runs over, the one named last changes fastest.
Arguments:
- latent_plane: bfloat16 [128, 2048, 512], P('ctx', 'expert'), may hold values from -64 to 64
- latent_rope: bfloat16 [128, 131072], P('ctx', 'expert'), may hold values from -7 to 7
- query_plane: bfloat16 [128, 128, 512], P('ctx', 'expert'), may hold values from -16 to 16
- query_rope: bfloat16 [128, 8192], P('ctx', 'expert'), may hold values from -32 to 32
- decode_hidden: bfloat16 [128, 7168], P('ctx', 'expert'), may hold values from -6 to 6
- lengths: int32 [32, 4], P('ctx'), may hold values from 128 to 2048, as said below
- owner: int32 [32, 4], P('ctx'), may hold values from 0 to 31, as said below
- norm_gain: float32 [7168], P('expert'), may hold values from 0.1 to 1.9
- routes: int32 [128, 8], P('ctx'), may hold values from 0 to 31, all different within a row; in each aligned block of 4 rows (0 to 3, 4 to 7, ...) at most 3 rows name the same one
- combine: float32 [128, 8], P('ctx'), may hold values from 0.1 to 1
- gate_weight: bfloat16 [32, 7168, 2048], P('ctx', None, 'expert'), may hold values from -0.0625 to 0.0625
- up_weight: bfloat16 [32, 7168, 2048], P('ctx', None, 'expert'), may hold values from -0.0625 to 0.0625
- down_weight: bfloat16 [32, 2048, 7168], P('ctx', 'expert'), may hold values from -0.125 to 0.125
Outputs:
- attended: bfloat16 [128, 65536], P('ctx', 'expert')
- moe_out: bfloat16 [128, 7168], P('ctx', 'expert')
The draws below stay inside these ranges and needn't reach their ends.
Inputs may be any that keep to these rules, and one draw needn't show every extreme that they name: Each row names 4 different owners, and every owner receives exactly 4 requests. `lengths`: each row sums to 4096, and its largest entry is 2048. `routes`: each row names 8 different experts; within the rows of one index of ctx no expert is named more than 3 times, and some expert reaches 3.
All inputs are finite; a program needn't handle non-finite values.
Results may differ from the reference program's by a relative error of at most 0.0091.
Values may be sent and summed in bfloat16 or wider, within the bound.
A program may use at most 128 MiB of HBM per device.

```python
import math
import jax
import jax.numpy as jnp
import numpy as np
from jax import lax

D = 7168
HEADS = 128
LAT = 512
ROPE = 64
FF_E = 2048
TOPK = 8
BLK = 128
L = 2048
REQ_DEV = 4
REQS = 128
WIN = 32
CAPX = 3
N_CTX = 32


def length_table(length_key):
    k_weights, k_order = jax.random.split(length_key, 2)
    shortest = max(1, L // 16)
    others = REQ_DEV - 2
    rest = REQ_DEV * L // 2 - L - shortest
    spread_total = rest - others * shortest
    weights = jax.random.randint(k_weights, (N_CTX, others), 1, 9).astype(jnp.int32)
    shares = shortest + spread_total * weights // jnp.sum(weights, axis=1, keepdims=True)
    deficit = rest - jnp.sum(shares, axis=1)
    shares = shares.at[:, 0].add(deficit)
    fixed_part = jnp.concatenate([jnp.full((N_CTX, 1), L, jnp.int32), jnp.full((N_CTX, 1), shortest, jnp.int32)], axis=1)
    table = jnp.concatenate([fixed_part, shares.astype(jnp.int32)], axis=1)
    order_scores = jax.random.randint(k_order, (N_CTX, REQ_DEV), 0, 1 << 20) * REQ_DEV + jnp.arange(REQ_DEV, dtype=jnp.int32)[None, :]
    order = jnp.argsort(order_scores, axis=1)
    return jnp.take_along_axis(table, order, axis=1).astype(jnp.int32)


def plant_site(key):
    request_lengths = length_table(jax.random.fold_in(key, 6)).reshape(REQS)
    raw = jax.random.randint(jax.random.fold_in(key, 7), (REQS,), 0, 1 << 20)
    span = request_lengths - 3
    return jnp.where(span >= 1, 2 + raw % jnp.maximum(span, 1), 0).astype(jnp.int32)


def latent_parts(key):
    keys = jax.random.split(key, 10)
    k_plane, k_rope, k_rows, k_near, k_rnear, k_pick, k_amp, k_sign, k_magn, k_prope = keys
    site = plant_site(key)
    positions = jnp.arange(L, dtype=jnp.int32)
    first = (positions[None, :] == site[:, None])[..., None]
    second = (positions[None, :] == site[:, None] + 1)[..., None]
    row_scale = jnp.exp(jax.random.uniform(k_rows, (REQS, L, 1), jnp.float32, 0.0, math.log(10.0)))
    row_scale = jnp.where(first, 1.0, row_scale)
    plane = jnp.clip(jax.random.normal(k_plane, (REQS, L, LAT), jnp.float32), -6.0, 6.0) * row_scale
    signs = jnp.where(jax.random.bernoulli(k_sign, 0.5, (REQS, 1, LAT)), 1.0, -1.0)
    plant = signs * jax.random.uniform(k_magn, (REQS, 1, LAT), jnp.float32, 2.5, 3.0)
    plane = jnp.where(first, plant, plane)
    plane = jnp.where(second, plane, plane)
    rope = jnp.clip(jax.random.normal(k_rope, (REQS, L, ROPE), jnp.float32), -6.0, 6.0)
    plant_rope = jnp.clip(jax.random.normal(k_prope, (REQS, 1, ROPE), jnp.float32), -6.0, 6.0)
    rope = jnp.where(first, plant_rope, rope)
    rope = jnp.where(second, rope, rope)
    picked = jax.random.bernoulli(k_pick, 1.0 / 16.0, (REQS, HEADS, 1))
    amplitude = jax.random.uniform(k_amp, (REQS, HEADS, 1), jnp.float32, 3.0, 5.0)
    return (plane, rope, plant, plant_rope, picked, amplitude)


def owner_table(owner_key):
    k_first, k_second, k_offset = jax.random.split(owner_key, 3)
    first_perm = jax.random.permutation(k_first, N_CTX)
    second_perm = jax.random.permutation(k_second, N_CTX)
    offsets = jax.random.permutation(k_offset, N_CTX)[:REQ_DEV]
    position = (second_perm[:, None] + offsets[None, :]) % N_CTX
    return first_perm[position].astype(jnp.int32)


def request_of_row(owner_key):
    owner_flat = owner_table(owner_key).reshape(REQS)
    onehot = (owner_flat[:, None] == jnp.arange(N_CTX, dtype=jnp.int32)[None, :]).astype(jnp.int32)
    before = jnp.cumsum(onehot, axis=0) - onehot
    ranking = jnp.sum(before * onehot, axis=1)
    target = (owner_flat * REQ_DEV + ranking).astype(jnp.int32)
    return jnp.zeros((REQS,), jnp.int32).at[target].set(jnp.arange(REQS, dtype=jnp.int32))


def draw_latent_plane(key, part):
    plane, rope, plant, plant_rope, picked, amplitude = latent_parts(key)
    return plane.astype(jnp.bfloat16)


def draw_latent_rope(key, part):
    plane, rope, plant, plant_rope, picked, amplitude = latent_parts(key)
    return rope.reshape(REQS, L * ROPE).astype(jnp.bfloat16)


def draw_query_plane(key, part):
    plane, rope, plant, plant_rope, picked, amplitude = latent_parts(key)
    source = request_of_row(jax.random.fold_in(key, 5))
    key = jax.random.fold_in(key, 3)
    base = jnp.clip(jax.random.normal(key, (REQS, HEADS, LAT), jnp.float32), -6.0, 6.0)
    values = jnp.where(picked, amplitude * plant[source], base)
    return values.astype(jnp.bfloat16)


def draw_query_rope(key, part):
    plane, rope, plant, plant_rope, picked, amplitude = latent_parts(key)
    source = request_of_row(jax.random.fold_in(key, 5))
    key = jax.random.fold_in(key, 4)
    base = jnp.clip(jax.random.normal(key, (REQS, HEADS, ROPE), jnp.float32), -6.0, 6.0)
    values = jnp.where(picked, amplitude * plant_rope[source], base)
    return values.reshape(REQS, HEADS * ROPE).astype(jnp.bfloat16)


def draw_owner(key, part):
    key = jax.random.fold_in(key, 5)
    return owner_table(key)


def draw_lengths(key, part):
    key = jax.random.fold_in(key, 6)
    return length_table(key)


def steps_of(own_key, extent, pieces, least, top_value):
    level, own = 1.0, jax.random.fold_in(own_key, 6)
    for axis_at, parts in pieces:
        heights = jnp.exp(jax.random.uniform(jax.random.fold_in(own, axis_at), (parts,), jnp.float32, least / len(pieces), top_value / len(pieces)))
        level = level * jnp.repeat(heights, extent[axis_at] // parts).reshape([-1 if axis == axis_at else 1 for axis in range(len(extent))])
    return level


def shared_out(own_key, own, number, rows, amount, top, bound, slope):
    sequence = jax.random.permutation(own_key, amount)
    crowded, ordinary = portions_of(amount, rows * top, bound, slope, True), portions_of(amount, rows * top, bound, slope, False)
    places = jnp.arange(amount)

    def named(sizes, offset_by):
        used = int((sizes > 0).sum())
        fixed = max(1, used // 4)
        passed = fixed + (places - fixed + offset_by * (used - fixed)) % max(1, amount - fixed)
        return jnp.zeros((amount,), jnp.int32).at[sequence[jnp.where(places < fixed, places, passed)]].set(jnp.asarray(sizes, jnp.int32))

    sizes = jnp.where(number % 4 == 0, named(crowded, number // 4), named(ordinary, number - number // 4 - 1))
    mixed = jax.random.permutation(jax.random.fold_in(own, 3), amount)
    donor, taker = mixed[0:amount // 2 * 2:2], mixed[1:amount // 2 * 2:2]
    slack = jnp.minimum(sizes[donor] - 1, bound - sizes[taker]) // 2
    slack = jnp.where((donor == sequence[0]) | (taker == sequence[0]) | (sizes[taker] == 0), 0, jnp.maximum(slack, 0))
    passed = jax.random.randint(jax.random.fold_in(own, 4), (amount // 2,), 0, 1 << 20) % (slack + 1)
    sizes = sizes.at[donor].add(-passed).at[taker].add(passed)
    items = jnp.searchsorted(jnp.cumsum(sizes), jnp.arange(rows * top), side="right").astype(jnp.int32)
    table = items.reshape(top, rows).T
    table = table[jax.random.permutation(jax.random.fold_in(own, 1), rows)]
    offset_by = jax.random.randint(jax.random.fold_in(own, 2), (rows, 1), 0, top)
    return jnp.take_along_axis(table, (jnp.arange(top)[None, :] + offset_by) % top, axis=1)


def portions_of(count, total, bound, lean, full):
    weights = [(1 << 20) // math.isqrt(grade ** lean) + 1 for grade in range(1, count + 1)]
    largest = bound if full else min(bound, max(-(-total // count), total * weights[0] // sum(weights)))
    least = 1 if total - largest >= count - 1 else 0
    given, surplus = [largest] + [least] * (count - 1), total - largest - least * (count - 1)
    while surplus > 0:
        candidates = [i for i in range(1, count) if given[i] < largest] or [i for i in range(1, count) if given[i] < bound]
        whole, budget = sum([weights[i] for i in candidates]), surplus
        for i in candidates:
            addition = min(bound - given[i], max(1, budget * weights[i] // whole), surplus)
            given[i] = given[i] + addition
            surplus = surplus - addition
    return np.array(given)


def normal_values(rng, shape, deviation, limit, cuts=(), held_as=jnp.bfloat16):
    loudness = steps_of(rng, shape, cuts, -0.22, 0.18) if cuts else 1.0
    array = jax.random.normal(rng, shape, jnp.float32) * deviation * loudness
    return jnp.minimum(jnp.maximum(array, -limit), limit).astype(held_as)


def setup_inputs(seed: int = 0) -> dict:
    streams_of = jax.random.split(jax.random.key(seed), 14)
    latent_plane = draw_latent_plane(jax.random.fold_in(streams_of[13], 71), 0)
    latent_rope = draw_latent_rope(jax.random.fold_in(streams_of[13], 71), 0)
    query_plane = draw_query_plane(jax.random.fold_in(streams_of[13], 71), 0)
    query_rope = draw_query_rope(jax.random.fold_in(streams_of[13], 71), 0)
    decode_hidden = normal_values(streams_of[4], (REQS, D), 1.0, 6.0, ((0, 32), (1, 8)))
    lengths = draw_lengths(jax.random.fold_in(streams_of[13], 71), 0)
    owner = draw_owner(jax.random.fold_in(streams_of[13], 71), 0)
    norm_gain = jnp.clip(1.0 + 0.18 * jax.random.normal(streams_of[7], (D,), jnp.float32), 0.1, 1.9)
    routes_keys = jax.random.split(jax.random.fold_in(streams_of[8], 1), REQS // REQ_DEV)
    routes_turns = jax.random.permutation(jax.random.fold_in(streams_of[8], 3), REQS // REQ_DEV)
    routes = jax.vmap(lambda own, number: shared_out(jax.random.fold_in(streams_of[8], 2), own, number, REQ_DEV, WIN, TOPK, CAPX, 2))(routes_keys, routes_turns).reshape((REQS, TOPK))
    combine = jnp.clip(jnp.exp(math.log(1.0) - 2.3025851 * jax.random.uniform(streams_of[9], (REQS, TOPK), jnp.float32) ** steps_of(streams_of[9], (REQS, TOPK), ((0, 32),), -0.2, 0.2)), 0.1, 1.0)
    gate_weight = normal_values(streams_of[10], (WIN, D, FF_E), D ** -0.5, 0.0625, ((0, 32), (2, 8)))
    up_weight = normal_values(streams_of[11], (WIN, D, FF_E), D ** -0.5, 0.0625, ((0, 32), (2, 8)))
    down_weight = normal_values(streams_of[12], (WIN, FF_E, D), FF_E ** -0.5, 0.125, ((0, 32), (1, 8)))
    return {"latent_plane": latent_plane, "latent_rope": latent_rope, "query_plane": query_plane, "query_rope": query_rope, "decode_hidden": decode_hidden, "lengths": lengths, "owner": owner, "norm_gain": norm_gain, "routes": routes, "combine": combine, "gate_weight": gate_weight, "up_weight": up_weight, "down_weight": down_weight}


score_scale = 192.0 ** (-0.5)
pack_limit = 448.0

def reference(latent_plane, latent_rope, query_plane, query_rope, decode_hidden, lengths, owner, norm_gain, routes, combine, gate_weight, up_weight, down_weight):
    blocks = latent_plane.astype(jnp.float32).reshape(REQS, L, LAT // BLK, BLK)
    scales = ((lax.optimization_barrier(jnp.max(jnp.abs(blocks), axis=-1)) + 1e-06) / pack_limit).astype(jnp.bfloat16)
    packed = (blocks / scales.astype(jnp.float32)[..., None]).astype(jnp.bfloat16)
    key_rows = (packed.astype(jnp.float32) * scales.astype(jnp.float32)[..., None]).reshape(REQS, L, LAT).astype(jnp.bfloat16)
    rope_rows = latent_rope.reshape(REQS, L, ROPE)
    visible = jnp.arange(L, dtype=jnp.int32)[None, :] < lengths.reshape(REQS)[:, None]
    owner_flat = owner.reshape(REQS)
    onehot = (owner_flat[:, None] == jnp.arange(N_CTX, dtype=jnp.int32)[None, :]).astype(jnp.int32)
    before = jnp.cumsum(onehot, axis=0) - onehot
    ranking = lax.optimization_barrier(jnp.sum(before * onehot, axis=1))
    target = (owner_flat * REQ_DEV + ranking).astype(jnp.int32)
    query_lat_all = query_plane[target]
    query_pos = query_rope.reshape(REQS, HEADS, ROPE)[target]

    def attend(inputs):
        query_lat, query_rot, key_lat, key_rot, seen = inputs
        scores = jnp.einsum('hc,pc->hp', query_lat.astype(jnp.float32), key_lat.astype(jnp.float32))
        scores = scores + jnp.einsum('he,pe->hp', query_rot.astype(jnp.float32), key_rot.astype(jnp.float32))
        scores = scores * score_scale
        masked = jnp.where(seen[None, :], scores, -jnp.inf)
        highest = lax.optimization_barrier(jnp.max(masked, axis=-1, keepdims=True))
        exponent = jnp.where(seen[None, :], jnp.exp(masked - highest), 0.0)
        totals = lax.optimization_barrier(jnp.sum(exponent, axis=-1, keepdims=True))
        probs = (exponent / totals).astype(jnp.bfloat16)
        return jnp.einsum('hp,pc->hc', probs.astype(jnp.float32), key_lat.astype(jnp.float32)).astype(jnp.bfloat16)
    attn = lax.map(attend, (query_lat_all, query_pos, key_rows, rope_rows, visible))
    attended = jnp.zeros((REQS, HEADS * LAT), jnp.bfloat16).at[target].set(attn.reshape(REQS, HEADS * LAT))
    stateful = decode_hidden.astype(jnp.float32)
    meansq = lax.optimization_barrier(jnp.mean(stateful * stateful, axis=-1, keepdims=True))
    normed = (stateful * lax.rsqrt(meansq + 1e-06) * norm_gain[None, :]).astype(jnp.bfloat16)

    def one_expert(totals, inputs):
        w_gate, w_up, w_down, index = inputs
        chosen = routes == index
        weight_rows = lax.optimization_barrier(jnp.sum(jnp.where(chosen, combine, 0.0), axis=1))
        picked = jnp.any(chosen, axis=1)
        ordering = jnp.argsort(jnp.where(picked, 0, 1).astype(jnp.int32), stable=True)[:N_CTX * CAPX].astype(jnp.int32)
        rows_in = normed[ordering]
        gate_act = jnp.dot(rows_in, w_gate, preferred_element_type=jnp.float32)
        up_act = jnp.dot(rows_in, w_up, preferred_element_type=jnp.float32)
        hidden = (jax.nn.silu(gate_act) * up_act).astype(jnp.bfloat16)
        result = jnp.dot(hidden, w_down, preferred_element_type=jnp.float32).astype(jnp.bfloat16)
        totals = totals.at[ordering].add(weight_rows[ordering][:, None] * result.astype(jnp.float32))
        return (totals, None)
    start = jnp.zeros((REQS, D), jnp.float32)
    summed, unused = lax.scan(one_expert, start, (gate_weight, up_weight, down_weight, jnp.arange(WIN, dtype=jnp.int32)))
    return (attended, summed.astype(jnp.bfloat16))
```

```python
import functools

import jax
import jax.numpy as jnp
from jax import lax
from jax.experimental import pallas as pl
from jax.experimental.pallas import tpu as pltpu
from jax.sharding import PartitionSpec as P

D = 7168
LAT = 512
ROPE = 64
BLK = 128
NX = 4
NZ = 8
NE = 8
NY = 4
REQ = 4
HD = 16
QW = 640
POS = 256
CAP = 3
SLOTS = NX * NZ * CAP
FEAT = D // NE
FF = 256

MESH = pl.DeviceIdType.MESH
BF = jnp.bfloat16
F32 = jnp.float32
score_scale = 192.0 ** (-0.5)
pack_limit = 448.0
HIDDEN_SCORE = -1e30


def coordinates():
    c = lax.axis_index("ctx")
    e = lax.axis_index("expert")
    return c, e, lax.div(c, NZ), lax.rem(c, NZ), lax.div(e, 2), lax.rem(e, 2)


def greet(peers):
    barrier = pltpu.get_barrier_semaphore()
    for peer in peers:
        pl.semaphore_signal(barrier, inc=1, device_id=peer, device_id_type=MESH)
    pl.semaphore_wait(barrier, len(peers))


def remote(src, dst, send_sem, recv_sem, peer):
    return pltpu.make_async_remote_copy(
        src_ref=src,
        dst_ref=dst,
        send_sem=send_sem,
        recv_sem=recv_sem,
        device_id=peer,
        device_id_type=MESH,
    )


class Ring:
    def __init__(self, buf, send, recv, x, z, e):
        self.buf, self.send, self.recv = buf, send, recv
        self.x, self.z, self.e = x, z, e
        self.copies = {}

    def step(self, s):
        for h in range(2):
            for way, sign in ((0, 1), (1, -1)):
                if s == 4 and h != way:
                    continue
                if s > 1:
                    self.copies[way, s - 1, h].wait_recv()
                origin = lax.rem(self.z + NZ - sign * (s - 1), NZ)
                block = self.buf.at[origin, pl.ds(2 * h, 2)]
                peer = (self.x * NZ + lax.rem(self.z + NZ + sign, NZ), self.e)
                n = (s - 1) * 4 + h * 2 + way
                copy = remote(block, block, self.send.at[n], self.recv.at[n], peer)
                copy.start()
                self.copies[way, s, h] = copy

    def finish(self):
        for way in range(2):
            self.copies[way, 3, 1 - way].wait_recv()
            self.copies[way, 4, way].wait_recv()
        for copy in self.copies.values():
            copy.wait_send()


def spread_kernel(
    q_ref, tok_ref, meta_ref, gain_ref,
    qz_ref, tk_ref, mt_ref, gn_ref,
    ring_s, ring_r, z_s, z_r, x_s, x_r, g_s, g_r,
):
    c, e, x, z, y, k = coordinates()

    def zp(d):
        return (x * NZ + lax.rem(z + d, NZ), e)

    def xp(d):
        return (lax.rem(x + d, NX) * NZ + z, e)

    def ep(d):
        return (c, lax.rem(e + d, NE))

    qz_ref[z] = q_ref[...]
    tk_ref[x, z] = tok_ref[...]
    mt_ref[x, z] = meta_ref[...]
    gn_ref[e] = gain_ref[...]
    greet([zp(d) for d in range(1, NZ)] + [xp(d) for d in range(1, NX)] + [ep(d) for d in range(1, NE)])
    z_copies = []
    for d in (1, 7, 2, 6, 3, 5, 4):
        z_copies.append(remote(meta_ref, mt_ref.at[x, z], z_s.at[0, d - 1], z_r.at[0, d - 1], zp(d)))
        z_copies.append(remote(tok_ref, tk_ref.at[x, z], z_s.at[1, d - 1], z_r.at[1, d - 1], zp(d)))
    for copy in z_copies:
        copy.start()
    ring = Ring(qz_ref, ring_s, ring_r, x, z, e)
    ring.step(1)
    gains = [remote(gain_ref, gn_ref.at[e], g_s.at[d - 1], g_r.at[d - 1], ep(d)) for d in range(1, NE)]
    for copy in gains:
        copy.start()
    ring.step(2)
    for copy in z_copies:
        copy.wait_recv()
    x_copies = []
    for d in range(1, NX):
        x_copies.append(remote(mt_ref.at[x], mt_ref.at[x], x_s.at[0, d - 1], x_r.at[0, d - 1], xp(d)))
        x_copies.append(remote(tk_ref.at[x], tk_ref.at[x], x_s.at[1, d - 1], x_r.at[1, d - 1], xp(d)))
    for copy in x_copies:
        copy.start()
    ring.step(3)
    ring.step(4)
    ring.finish()
    for copy in x_copies + gains:
        copy.wait_recv()
    for copy in z_copies + x_copies + gains:
        copy.wait_send()


def spread(q, tok, meta, gain):
    vmem = pl.BlockSpec(memory_space=pltpu.VMEM)
    dma = pltpu.SemaphoreType.DMA
    return pl.pallas_call(
        spread_kernel,
        out_shape=(
            jax.ShapeDtypeStruct((NZ,) + q.shape, q.dtype),
            jax.ShapeDtypeStruct((NX, NZ) + tok.shape, tok.dtype),
            jax.ShapeDtypeStruct((NX, NZ) + meta.shape, meta.dtype),
            jax.ShapeDtypeStruct((NE,) + gain.shape, gain.dtype),
        ),
        in_specs=[vmem] * 4,
        out_specs=(vmem,) * 4,
        scratch_shapes=[
            dma((16,)), dma((16,)),
            dma((2, 7)), dma((2, 7)),
            dma((2, 3)), dma((2, 3)),
            dma((7,)), dma((7,)),
        ],
        compiler_params=pltpu.CompilerParams(
            collective_id=0, has_side_effects=True, vmem_limit_bytes=16 * 1024 * 1024
        ),
    )(q, tok, meta, gain)


def layer_kernel(
    idx_ref, qz_ref, xt_ref, gain_ref, whi_ref, wlo_ref, rope_ref,
    lat_hbm, wg_hbm, wu_hbm, wd_hbm,
    att_ref, moe_ref,
    wg, wu, wd, lat, kcat, xbuf, xsend, qall, tall, xn, osend, orecv,
    ysib, ysr, yown, ysend, yrecv, xrs, xrr, zs, zr, og, oxs, oxr,
    w_sem, qx_s, qx_r, qy_s, qy_r, qk_s, qk_r, ty_s, ty_r, tk_s, tk_r,
    o_s, o_r, yk_s, yk_r, yy_s, yy_r, xr_s, xr_r, zr_s, zr_r, ring_s, ring_r, ox_s, ox_r,
):
    c, e, x, z, y, k = coordinates()

    def zp(d):
        return (x * NZ + lax.rem(z + d, NZ), e)

    def xp(d):
        return (lax.rem(x + d, NX) * NZ + z, e)

    def ep(d):
        return (c, lax.rem(e + d, NE))

    def yp(d):
        return (c, lax.rem(y + d, NY) * 2 + k)

    sib = (c, y * 2 + 1 - k)

    loads = [
        pltpu.make_async_copy(lat_hbm, lat, w_sem.at[0]),
        pltpu.make_async_copy(wg_hbm.at[0], wg, w_sem.at[1]),
        pltpu.make_async_copy(wu_hbm.at[0], wu, w_sem.at[2]),
        pltpu.make_async_copy(wd_hbm.at[0], wd, w_sem.at[3]),
    ]
    for load in loads:
        load.start()
    greet([zp(d) for d in range(1, NZ)] + [xp(d) for d in range(1, NX)] + [ep(d) for d in range(1, NE)])

    qx = []
    for d in range(1, NX):
        target = lax.rem(x + d, NX)
        for j in range(REQ):
            xsend[d - 1, j] = qz_ref[idx_ref[target * REQ + j]]
        qx.append(remote(xsend.at[d - 1], xbuf.at[x], qx_s.at[d - 1], qx_r.at[d - 1], xp(d)))
        qx[-1].start()
    for j in range(REQ):
        xbuf[x, j] = qz_ref[idx_ref[x * REQ + j]]

    ty = [remote(xt_ref, tall.at[e], ty_s.at[d - 1], ty_r.at[d - 1], yp(d)) for d in range(1, NY)]
    tk = [remote(xt_ref, tall.at[e], tk_s.at[0], tk_r.at[0], sib)]
    for copy in ty + tk:
        copy.start()
    tall[e] = xt_ref[...]

    for copy in qx:
        copy.wait_recv()
    for j in range(REQ):
        qall[j, e] = xbuf[idx_ref[16 + j], j]
    mine = qall.at[:, e]
    qy = [remote(mine, mine, qy_s.at[d - 1], qy_r.at[d - 1], yp(d)) for d in range(1, NY)]
    qk = [remote(mine, mine, qk_s.at[0], qk_r.at[0], sib)]
    for copy in qy + qk:
        copy.start()

    loads[0].wait()
    for j in range(REQ):
        for b in range(LAT // BLK):
            block = lat[j, :, b * BLK:(b + 1) * BLK].astype(F32)
            scale = ((jnp.max(jnp.abs(block), axis=-1, keepdims=True) + 1e-06) / pack_limit).astype(BF)
            scale = scale.astype(F32)
            packed = (block / scale).astype(BF)
            kcat[j, :, b * BLK:(b + 1) * BLK] = (packed.astype(F32) * scale).astype(BF)
        kcat[j, :, LAT:] = rope_ref[j]

    for d in range(1, NY):
        qy[d - 1].wait_recv()
        other = lax.rem(y + NY - d, NY) * 2 + k
        copy = remote(qall.at[:, other], qall.at[:, other], qk_s.at[d], qk_r.at[d], sib)
        copy.start()
        qk.append(copy)
    for d in range(1, NY):
        ty[d - 1].wait_recv()
        other = lax.rem(y + NY - d, NY) * 2 + k
        copy = remote(tall.at[other], tall.at[other], tk_s.at[d], tk_r.at[d], sib)
        copy.start()
        tk.append(copy)
    for copy in qk:
        copy.wait_recv()

    lanes = lax.broadcasted_iota(jnp.int32, (1, POS), 1) + e * POS
    side = lax.broadcasted_iota(jnp.int32, (HD * NE, QW - LAT), 1)
    for j in range(REQ):
        scores = lax.dot_general(
            qall[j].reshape(NE * HD, QW), kcat[j], (((1,), (1,)), ((), ())), preferred_element_type=F32
        )
        scores = jnp.where(lanes < idx_ref[20 + j], scores * score_scale, HIDDEN_SCORE)
        highest = jnp.max(scores, axis=-1, keepdims=True)
        weights = jnp.exp(scores - highest)
        total = jnp.sum(weights, axis=-1, keepdims=True)
        out = jnp.dot(weights.astype(BF), kcat[j, :, :LAT], preferred_element_type=F32) / total
        level = highest + jnp.log(total)
        first = level.astype(BF).astype(F32)
        second = (level - first).astype(BF).astype(F32)
        third = level - first - second
        tail = jnp.where(side == 0, first, jnp.where(side == 1, second, jnp.where(side == 2, third, 0.0)))
        osend[:, j, :, :LAT] = out.astype(BF).reshape(NE, HD, LAT)
        osend[:, j, :, LAT:] = tail.astype(BF).reshape(NE, HD, QW - LAT)
    oc = []
    for d in range(1, NE):
        copy = remote(osend.at[lax.rem(e + d, NE)], orecv.at[e], o_s.at[d - 1], o_r.at[d - 1], ep(d))
        copy.start()
        oc.append(copy)
    orecv[e] = osend[e]

    for copy in tk:
        copy.wait_recv()
    squares = jnp.zeros((SLOTS, 1), F32)
    for g in range(NE):
        rows = tall[g].astype(F32)
        squares = squares + jnp.sum(rows * rows, axis=-1, keepdims=True)
    inverse = lax.rsqrt(squares / D + 1e-06)
    for g in range(NE):
        xn[g] = (tall[g].astype(F32) * inverse * gain_ref[:, g * FEAT:(g + 1) * FEAT]).astype(BF)
    for load in loads[1:]:
        load.wait()
    gate = jnp.zeros((SLOTS, FF), F32)
    up = jnp.zeros((SLOTS, FF), F32)
    for g in range(NE):
        gate = gate + jnp.dot(xn[g], wg[g * FEAT:(g + 1) * FEAT, :], preferred_element_type=F32)
        up = up + jnp.dot(xn[g], wu[g * FEAT:(g + 1) * FEAT, :], preferred_element_type=F32)
    hidden = (jax.nn.silu(gate) * up).astype(BF)

    def project(target):
        columns = pl.ds(pl.multiple_of(target * FEAT, BLK), FEAT)
        return jnp.dot(hidden, wd[:, columns], preferred_element_type=F32)

    yk = []
    for d in range(NY):
        target = lax.rem(y + d + 1, NY) * 2 + 1 - k
        ysib[d] = project(target).astype(BF)
        copy = remote(ysib.at[d], ysr.at[d], yk_s.at[d], yk_r.at[d], sib)
        copy.start()
        yk.append(copy)
    for d in range(NY):
        yown[d] = project(lax.rem(y + d + 1, NY) * 2 + k)
    yy = []
    for d in range(NY - 1):
        yk[d].wait_recv()
        ysend[d] = (yown[d] + ysr[d].astype(F32)).astype(BF)
        copy = remote(ysend.at[d], yrecv.at[d], yy_s.at[d], yy_r.at[d], yp(d + 1))
        copy.start()
        yy.append(copy)

    for copy in oc:
        copy.wait_recv()
    for j in range(REQ):
        levels = [jnp.sum(orecv[g, j, :, LAT:].astype(F32), axis=-1, keepdims=True) for g in range(NE)]
        top = functools.reduce(jnp.maximum, levels)
        share = [jnp.exp(level - top) for level in levels]
        total = functools.reduce(jnp.add, share)
        acc = share[0] * orecv[0, j, :, :LAT].astype(F32)
        for g in range(1, NE):
            acc = acc + share[g] * orecv[g, j, :, :LAT].astype(F32)
        og[z, j] = (acc / total).astype(BF)
    ring = Ring(og, ring_s, ring_r, x, z, e)
    ring.step(1)

    yk[NY - 1].wait_recv()
    summed = yown[NY - 1] + ysr[NY - 1].astype(F32)
    for copy in yy:
        copy.wait_recv()
    for d in range(NY - 1):
        summed = summed + yrecv[d].astype(F32)
    rounded = summed.astype(BF)

    def weighted(target):
        rows = pl.ds(pl.multiple_of(target * 32, 32), 32)
        return jnp.dot(whi_ref[rows, :], rounded, preferred_element_type=F32) + jnp.dot(
            wlo_ref[rows, :], rounded, preferred_element_type=F32
        )

    xr = []
    for d in range(1, NX):
        xrs[d - 1] = weighted(lax.rem(x + d, NX)).astype(BF)
        copy = remote(xrs.at[d - 1], xrr.at[d - 1], xr_s.at[d - 1], xr_r.at[d - 1], xp(d))
        copy.start()
        xr.append(copy)
    own = weighted(x)
    ring.step(2)
    for copy in xr:
        copy.wait_recv()
    for d in range(NX - 1):
        own = own + xrr[d].astype(F32)
    for t in range(NZ):
        zs[t, 0:4, 0:512] = own[4 * t:4 * t + 4, 0:512]
        zs[t, 4:8, 0:384] = own[4 * t:4 * t + 4, 512:896]
        zs[t, 4:8, 384:512] = jnp.zeros((4, 128), F32)
    zc = []
    for d in range(1, NZ):
        copy = remote(zs.at[lax.rem(z + d, NZ)], zr.at[d - 1], zr_s.at[d - 1], zr_r.at[d - 1], zp(d))
        copy.start()
        zc.append(copy)
    ring.step(3)
    ring.step(4)
    for copy in zc:
        copy.wait_recv()
    final = zs[z]
    for d in range(NZ - 1):
        final = final + zr[d]
    moe_ref[:, 0:512] = final[0:4, :].astype(BF)
    moe_ref[:, 512:896] = final[4:8, 0:384].astype(BF)
    ring.finish()

    ox = []
    for d in range(1, NX):
        target = lax.rem(x + d, NX)
        for j in range(REQ):
            at = idx_ref[24 + target * REQ + j]
            oxs[d - 1, j] = og[at // REQ, at % REQ]
        ox.append(remote(oxs.at[d - 1], oxr.at[x], ox_s.at[d - 1], ox_r.at[d - 1], xp(d)))
        ox[-1].start()
    for j in range(REQ):
        at = idx_ref[24 + x * REQ + j]
        oxr[x, j] = og[at // REQ, at % REQ]
    for copy in ox:
        copy.wait_recv()
    for j in range(REQ):
        att_ref[j] = oxr[idx_ref[40 + j], j]
    for copy in qx + ty + tk + qy + qk + oc + yk + yy + xr + zc + ox:
        copy.wait_send()


def layer(idx, qz, xt, gain, whi, wlo, rope, lat, wg, wu, wd):
    vmem = pl.BlockSpec(memory_space=pltpu.VMEM)
    hbm = pl.BlockSpec(memory_space=pl.ANY)
    dma = pltpu.SemaphoreType.DMA
    V = pltpu.VMEM
    pairs = []
    for count in (3, 3, 4, 3, 4, 7, 4, 3, 3, 7, 16, 3):
        pairs += [dma((count,)), dma((count,))]
    return pl.pallas_call(
        layer_kernel,
        out_shape=(
            jax.ShapeDtypeStruct((REQ, HD, LAT), BF),
            jax.ShapeDtypeStruct((REQ, FEAT), BF),
        ),
        in_specs=[pl.BlockSpec(memory_space=pltpu.SMEM)] + [vmem] * 6 + [hbm] * 4,
        out_specs=(vmem, vmem),
        scratch_shapes=[
            V((D, FF), BF), V((D, FF), BF), V((FF, D), BF),
            V((REQ, POS, LAT), BF), V((REQ, POS, QW), BF),
            V((NX, REQ, HD, QW), BF), V((NX - 1, REQ, HD, QW), BF),
            V((REQ, NE, HD, QW), BF),
            V((NE, SLOTS, FEAT), BF), V((NE, SLOTS, FEAT), BF),
            V((NE, REQ, HD, QW), BF), V((NE, REQ, HD, QW), BF),
            V((NY, SLOTS, FEAT), BF), V((NY, SLOTS, FEAT), BF), V((NY, SLOTS, FEAT), F32),
            V((NY - 1, SLOTS, FEAT), BF), V((NY - 1, SLOTS, FEAT), BF),
            V((NX - 1, 32, FEAT), BF), V((NX - 1, 32, FEAT), BF),
            V((NZ, 8, 512), F32), V((NZ - 1, 8, 512), F32),
            V((NZ, REQ, HD, LAT), BF),
            V((NX - 1, REQ, HD, LAT), BF), V((NX, REQ, HD, LAT), BF),
            dma((4,)),
        ] + pairs,
        compiler_params=pltpu.CompilerParams(
            collective_id=1, has_side_effects=True, vmem_limit_bytes=48 * 1024 * 1024
        ),
    )(idx, qz, xt, gain, whi, wlo, rope, lat, wg, wu, wd)


def local(
    latent_plane,
    latent_rope,
    query_plane,
    query_rope,
    decode_hidden,
    lengths,
    owner,
    norm_gain,
    routes,
    combine,
    gate_weight,
    up_weight,
    down_weight,
):
    c, e, x, z, y, k = coordinates()
    experts = NX * NZ
    q = jnp.concatenate(
        [query_plane, query_rope.reshape(REQ, HD, ROPE), jnp.zeros((REQ, HD, QW - LAT - ROPE), BF)], axis=-1
    )
    tok = jnp.pad(decode_hidden, ((0, 0), (0, 128))).reshape(REQ, 4, 256).transpose(1, 0, 2).reshape(16, 256)
    named = routes[:, :, None] == jnp.arange(experts, dtype=jnp.int32)[None, None, :]
    dense = jnp.sum(jnp.where(named, combine[:, :, None], 0.0), axis=1)
    request = jnp.stack([owner[0], lengths[0]], axis=1).astype(F32)
    meta = jnp.concatenate(
        [jnp.pad(dense, ((0, 0), (0, 96))), jnp.pad(request, ((0, 0), (0, 126)))], axis=0
    )
    gain = jnp.pad(norm_gain.reshape(7, 128), ((0, 1), (0, 0)))
    rope = jnp.pad(latent_rope.reshape(REQ, POS, ROPE), ((0, 0), (0, 0), (0, QW - LAT - ROPE)))

    qz, tk, mt, gn = spread(q, tok, meta, gain)

    mt = mt.reshape(experts, 8, 128)
    gain_all = gn[:, :7].reshape(1, D)
    owners = mt[:, 4:, 0].astype(jnp.int32).reshape(experts * REQ)
    number = jnp.arange(experts * REQ, dtype=jnp.int32)
    rank = jnp.sum((owners[:, None] == owners[None, :]) & (number[None, :] < number[:, None]), axis=1).astype(jnp.int32)
    row = owners * REQ + rank
    request_of = jnp.sum(jnp.where(row[None, :] == number[:, None], number[None, :], 0), axis=1)
    here = ((number // REQ) % NZ) == z

    def at_z(values):
        return jnp.sum(jnp.where(here, values, 0).reshape(NX, NZ, REQ), axis=1).reshape(NX * REQ)

    def at_c(values):
        return lax.dynamic_slice(values, (c * REQ,), (REQ,))

    idx = jnp.concatenate(
        [
            at_z((owners % NZ) * REQ + rank),
            at_c(owners // NZ),
            lengths[0],
            at_z(((request_of // REQ) % NZ) * REQ + request_of % REQ),
            at_c(request_of // (REQ * NZ)),
        ]
    ).astype(jnp.int32)

    lane = jnp.arange(128, dtype=jnp.int32) == c
    share = jnp.sum(jnp.where(lane, mt[:, :4, :], 0.0), axis=-1)
    chosen = share > 0
    count = chosen.astype(jnp.int32)
    before = jnp.sum(
        jnp.where(jnp.arange(REQ)[None, :, None] > jnp.arange(REQ)[None, None, :], count[:, None, :], 0), axis=2
    )
    slot = (jnp.arange(experts, dtype=jnp.int32)[:, None] * CAP + before).reshape(experts * REQ)
    slot = jnp.where(chosen.reshape(-1), slot, -1)
    placing = jnp.arange(SLOTS, dtype=jnp.int32)[:, None] == slot[None, :]
    flat = share.reshape(-1)
    high = flat.astype(BF).astype(F32)
    back = jnp.arange(SLOTS, dtype=jnp.int32)[None, :] == slot[:, None]
    whi = jnp.where(back, high[:, None], 0.0).astype(BF)
    wlo = jnp.where(back, (flat - high)[:, None], 0.0).astype(BF)
    tokens = tk.reshape(experts, 4, REQ, 256).transpose(0, 2, 1, 3).reshape(experts * REQ, 1024)[:, :FEAT]
    xt = jnp.dot(placing.astype(BF), tokens, preferred_element_type=F32).astype(BF)

    att, moe = layer(
        idx, qz.reshape(NZ * REQ, HD, QW), xt, gain_all, whi, wlo, rope,
        latent_plane, gate_weight, up_weight, down_weight,
    )
    return att.reshape(REQ, HD * LAT), moe


def solution(mesh):
    placed = (
        P("ctx", "expert", None),
        P("ctx", "expert"),
        P("ctx", "expert", None),
        P("ctx", "expert"),
        P("ctx", "expert"),
        P("ctx", None),
        P("ctx", None),
        P("expert"),
        P("ctx", None),
        P("ctx", None),
        P("ctx", None, "expert"),
        P("ctx", None, "expert"),
        P("ctx", "expert", None),
    )
    return jax.shard_map(
        local,
        mesh=mesh,
        in_specs=placed,
        out_specs=(P("ctx", "expert"), P("ctx", "expert")),
        check_vma=False,
    )
```

```python
import functools

import jax
import jax.numpy as jnp
from jax import lax
from jax.experimental import pallas as pl
from jax.experimental.pallas import tpu as pltpu
from jax.sharding import PartitionSpec as P

D = 7168
LAT = 512
ROPE = 64
BLK = 128
NX = 4
NZ = 8
NE = 8
NY = 4
REQ = 4
HD = 16
QW = 640
POS = 256
CAP = 3
SLOTS = NX * NZ * CAP
FEAT = D // NE
FF = 256

MESH = pl.DeviceIdType.MESH
BF = jnp.bfloat16
F32 = jnp.float32
score_scale = 192.0 ** (-0.5)
pack_limit = 448.0
HIDDEN_SCORE = -1e30


def coordinates():
    c = lax.axis_index("ctx")
    e = lax.axis_index("expert")
    return c, e, lax.div(c, NZ), lax.rem(c, NZ), lax.div(e, 2), lax.rem(e, 2)


def greet(peers):
    barrier = pltpu.get_barrier_semaphore()
    for peer in peers:
        pl.semaphore_signal(barrier, inc=1, device_id=peer, device_id_type=MESH)
    return lambda: pl.semaphore_wait(barrier, len(peers))


def remote(src, dst, send_sem, recv_sem, peer):
    return pltpu.make_async_remote_copy(
        src_ref=src,
        dst_ref=dst,
        send_sem=send_sem,
        recv_sem=recv_sem,
        device_id=peer,
        device_id_type=MESH,
    )


class Gather:
    def __init__(self, buf, send, recv, x, z, e):
        self.buf, self.send, self.recv = buf, send, recv
        self.x, self.z, self.e = x, z, e
        self.copies = {}

    def put(self, origin, hop, sign, low):
        block = self.buf.at[lax.rem(self.z + 2 * NZ - sign * origin, NZ), pl.ds(low, 2)]
        peer = (self.x * NZ + lax.rem(self.z + 2 * NZ + sign * hop, NZ), self.e)
        n = len(self.copies)
        copy = remote(block, block, self.send.at[n], self.recv.at[n], peer)
        copy.start()
        self.copies[origin + hop, sign, low] = copy

    def start(self):
        for hop in (2, 1):
            for low in (0, 2):
                for sign in (1, -1):
                    self.put(0, hop, sign, low)

    def forward(self):
        for first in (True, False):
            for sign in (1, -1):
                low = 0 if first == (sign == 1) else 2
                self.copies[2, sign, low].wait_recv()
                if first:
                    self.put(2, 2, sign, low)
                self.put(2, 1, sign, low)

    def finish(self):
        for (distance, sign, low), copy in self.copies.items():
            if distance != 2:
                copy.wait_recv()

    def drain(self):
        for copy in self.copies.values():
            copy.wait_send()


def three_parts(level, side):
    first = level.astype(BF).astype(F32)
    second = (level - first).astype(BF).astype(F32)
    third = level - first - second
    return jnp.where(side == 0, first, jnp.where(side == 1, second, jnp.where(side == 2, third, 0.0))).astype(BF)


def merge(parts):
    levels = [jnp.sum(part[:, LAT:].astype(F32), axis=-1, keepdims=True) for part in parts]
    top = functools.reduce(jnp.maximum, levels)
    share = [jnp.exp(level - top) for level in levels]
    total = functools.reduce(jnp.add, share)
    acc = share[0] * parts[0][:, :LAT].astype(F32)
    for weight, part in zip(share[1:], parts[1:]):
        acc = acc + weight * part[:, :LAT].astype(F32)
    return acc / total, top + jnp.log(total)


def bits(number, shift, count):
    return jnp.bitwise_and(jnp.right_shift(number, shift), count - 1)


def iota(shape, axis):
    return lax.broadcasted_iota(jnp.int32, shape, axis)


def layer_kernel(
    owner_ref, length_ref, routes_ref, combine_ref,
    q_ref, qr_ref, tok_ref, gain_ref, rope_ref,
    lat_hbm, wg_hbm, wu_hbm, wd_hbm,
    att_ref, moe_ref,
    table, wg, wu, wd, lat, kcat, qz, xbuf, xsend, qall, xt, tall, xn, opart, osib, omine, oin,
    ysib, ysr, yown, ysend, yrecv, tw, xrs, xrr, zs, zr, og, oxs, oxr, af,
    tokf, tokb, tk, gall, mzs, mzr, mxs, mxr, mrow, owz, owx, tbl, phi, plo,
    w_sem, t_sem, mz_s, mz_r, oz_s, oz_r, kz_s, kz_r, mx_s, mx_r, wx_s, wx_r, kx_s, kx_r, g_s, g_r,
    qz_s, qz_r, qx_s, qx_r, qy_s, qy_r, qk_s, qk_r, ty_s, ty_r, tk_s, tk_r,
    os_s, os_r, o_s, o_r, yk_s, yk_r, yy_s, yy_r, xr_s, xr_r, zr_s, zr_r, og_s, og_r, ox_s, ox_r,
):
    c, e, x, z, y, k = coordinates()
    pending = []

    def zp(d):
        return (x * NZ + lax.rem(z + d, NZ), e)

    def xp(d):
        return (lax.rem(x + d, NX) * NZ + z, e)

    def ep(d):
        return (c, lax.rem(e + d, NE))

    def yp(d):
        return (c, lax.rem(y + d, NY) * 2 + k)

    sib = (c, y * 2 + 1 - k)

    def start(src, dst, send_sem, recv_sem, peer):
        copy = remote(src, dst, send_sem, recv_sem, peer)
        copy.start()
        pending.append(copy)
        return copy

    loads = [
        pltpu.make_async_copy(lat_hbm, lat, w_sem.at[0]),
        pltpu.make_async_copy(wg_hbm.at[0], wg, w_sem.at[1]),
        pltpu.make_async_copy(wu_hbm.at[0], wu, w_sem.at[2]),
        pltpu.make_async_copy(wd_hbm.at[0], wd, w_sem.at[3]),
    ]
    loads[0].start()
    wait_for_all = greet(
        [zp(d) for d in range(1, NZ)] + [xp(d) for d in range(1, NX)] + [ep(d) for d in range(1, NE)]
    )
    for load in loads[1:]:
        load.start()

    lane = iota((8, 128), 1)
    mine = jnp.zeros((8, 128), jnp.int32)
    for j in range(REQ):
        mine = jnp.where(lane == c * REQ + j, owner_ref[0, j], mine)
    owz[z] = mine
    row = iota((64, 128), 0)
    expert = jnp.bitwise_and(row, 7) * NZ + jnp.right_shift(row, 3)
    wide = iota((64, 128), 1)
    weights = jnp.zeros((64, 128), F32)
    for j in range(REQ):
        for n in range(8):
            hit = (expert == routes_ref[j, n]) & (wide == c * REQ + j)
            weights = jnp.where(hit, combine_ref[j, n], weights)
    mzs[...] = weights.reshape(8, 8, 128)
    state = tok_ref[...].astype(F32)
    for g in range(4):
        width = 256 if g < 3 else 128
        tokf[4 * g:4 * g + 4, 0:width] = state[:, g * 256:g * 256 + width]
    tokf[12:16, 128:256] = jnp.zeros((4, 128), F32)
    tokb[...] = tokf[...].astype(BF)
    gall[e] = gain_ref[...]
    qz[z, :, :, 0:LAT] = q_ref[...]
    turned = jnp.concatenate(
        [
            jnp.where(
                jnp.right_shift(iota((HD, HD * ROPE), 1), 6) == iota((HD, HD * ROPE), 0),
                jnp.broadcast_to(qr_ref[...].astype(F32)[j:j + 1, :], (HD, HD * ROPE)),
                0.0,
            )
            for j in range(REQ)
        ],
        axis=0,
    ).astype(BF)
    fold = (jnp.bitwise_and(iota((HD * ROPE, 128), 0), 63) == iota((HD * ROPE, 128), 1)).astype(F32).astype(BF)
    qz[z, :, :, LAT:] = jnp.dot(turned, fold, preferred_element_type=F32).astype(BF).reshape(REQ, HD, 128)

    wait_for_all()
    around = (1, 7, 2, 6, 3, 5, 4)
    oz = [start(owz.at[z], owz.at[z], oz_s.at[d - 1], oz_r.at[d - 1], zp(d)) for d in around]
    mz = [
        start(mzs.at[lax.rem(z + d, NZ)], mzr.at[z], mz_s.at[d - 1], mz_r.at[d - 1], zp(d)) for d in around
    ]
    kz = [start(tokb, tk.at[x, z], kz_s.at[d - 1], kz_r.at[d - 1], zp(d)) for d in around]
    gather = Gather(qz, qz_s, qz_r, x, z, e)
    gather.start()
    gains = [start(gain_ref, gall.at[e], g_s.at[d - 1], g_r.at[d - 1], ep(d)) for d in range(1, NE)]
    mzr[z] = mzs[z]
    tk[x, z] = tokb[...]

    loads[0].wait()
    for j in range(REQ):
        for b in range(LAT // BLK):
            block = lat[j, :, b * BLK:(b + 1) * BLK].astype(F32)
            scale = ((jnp.max(jnp.abs(block), axis=-1, keepdims=True) + 1e-06) / pack_limit).astype(BF)
            scale = scale.astype(F32)
            packed = (block / scale).astype(BF)
            kcat[j, :, b * BLK:(b + 1) * BLK] = (packed.astype(F32) * scale).astype(BF)
        kcat[j, :, LAT:] = rope_ref[j]

    for copy in oz + mz:
        copy.wait_recv()
    owx[x] = functools.reduce(jnp.add, [owz[d] for d in range(NZ)])
    mxs[...] = functools.reduce(jnp.add, [mzr[d] for d in range(NZ)])
    mxr[x] = mxs[...]
    wx = [start(owx.at[x], owx.at[x], wx_s.at[d - 1], wx_r.at[d - 1], xp(d)) for d in range(1, NX)]
    mx = [start(mxs, mxr.at[x], mx_s.at[d - 1], mx_r.at[d - 1], xp(d)) for d in range(1, NX)]
    for copy in kz:
        copy.wait_recv()
    kx = [start(tk.at[x], tk.at[x], kx_s.at[d - 1], kx_r.at[d - 1], xp(d)) for d in range(1, NX)]
    gather.forward()

    for copy in wx + mx:
        copy.wait_recv()
    sub = iota((128, 128), 0)
    col = iota((128, 128), 1)
    owners = functools.reduce(jnp.add, [owx[d] for d in range(NX)])[0:1, :]
    across = jnp.broadcast_to(owners, (128, 128))
    rank = jnp.sum(jnp.where((across.T == across) & (sub < col), 1, 0), axis=0, keepdims=True)
    place = jnp.broadcast_to(owners * REQ + rank, (128, 128)).T
    request_of = jnp.sum(jnp.where(place == col, sub, 0), axis=0, keepdims=True)
    eight = iota((8, 128), 0)
    tbl[...] = jnp.where(eight == 0, owners, jnp.where(eight == 1, rank, request_of))
    to_scalars = pltpu.make_async_copy(tbl, table, t_sem.at[0])
    to_scalars.start()

    mrow[...] = functools.reduce(jnp.add, [mxr[d] for d in range(NX)])
    share = mrow[pl.ds(x, 1), :]
    chosen = jnp.where(share > 0, 1.0, 0.0)
    earlier = ((jnp.right_shift(sub, 2) == jnp.right_shift(col, 2)) & (sub < col)).astype(F32).astype(BF)
    before = jnp.dot(jnp.broadcast_to(chosen, (8, 128)).astype(BF), earlier, preferred_element_type=F32)[0:1, :]
    slot = (jnp.right_shift(iota((1, 128), 1), 2) * CAP).astype(F32) + before
    placing = jnp.where(iota((SLOTS, 128), 0).astype(F32) == slot, chosen, 0.0)
    scaled = placing * share
    high = scaled.astype(BF)
    phi[...] = high
    plo[...] = (scaled - high.astype(F32)).astype(BF)
    token_of = iota((128, 512), 1)
    token_of = jnp.right_shift(token_of, 4) * REQ + jnp.bitwise_and(token_of, 3)
    widen = (token_of == iota((128, 512), 0)).astype(F32).astype(BF)
    placing = jnp.dot(placing.astype(BF), widen, preferred_element_type=F32)
    group = jnp.bitwise_and(jnp.right_shift(iota((SLOTS, 512), 1), 2), 3)
    for copy in kx:
        copy.wait_recv()
    states = tk[...].reshape(512, 256)
    for g in range(4):
        width = 256 if g < 3 else 128
        part = jnp.where(group == g, placing, 0.0).astype(BF)
        xt[:, g * 256:g * 256 + width] = jnp.dot(
            part, states[:, 0:width], preferred_element_type=F32
        ).astype(BF)

    ty = [start(xt, tall.at[e], ty_s.at[d - 1], ty_r.at[d - 1], yp(d)) for d in range(1, NY)]
    tc = [start(xt, tall.at[e], tk_s.at[0], tk_r.at[0], sib)]
    tall[e] = xt[...]

    gather.finish()
    to_scalars.wait()
    qx = []
    for d in range(1, NX):
        target = lax.rem(x + d, NX)
        for j in range(REQ):
            r = (target * NZ + z) * REQ + j
            xsend[d - 1, j] = qz[bits(table[0, r], 0, NZ), bits(table[1, r], 0, REQ)]
        qx.append(start(xsend.at[d - 1], xbuf.at[x], qx_s.at[d - 1], qx_r.at[d - 1], xp(d)))
    for j in range(REQ):
        r = c * REQ + j
        xbuf[x, j] = qz[bits(table[0, r], 0, NZ), bits(table[1, r], 0, REQ)]

    for copy in qx:
        copy.wait_recv()
    for j in range(REQ):
        qall[j, e] = xbuf[bits(table[0, c * REQ + j], 3, NX), j]
    own = qall.at[:, e]
    qy = [start(own, own, qy_s.at[d - 1], qy_r.at[d - 1], yp(d)) for d in range(1, NY)]
    qk = [start(own, own, qk_s.at[0], qk_r.at[0], sib)]
    for d in range(1, NY):
        ty[d - 1].wait_recv()
        other = lax.rem(y + NY - d, NY) * 2 + k
        tc.append(start(tall.at[other], tall.at[other], tk_s.at[d], tk_r.at[d], sib))
    for d in range(1, NY):
        qy[d - 1].wait_recv()
        other = lax.rem(y + NY - d, NY) * 2 + k
        block = qall.at[:, other]
        qk.append(start(block, block, qk_s.at[d], qk_r.at[d], sib))
    for copy in qk:
        copy.wait_recv()

    lanes = iota((1, POS), 1) + e * POS
    side = iota((HD * NE, QW - LAT), 1)
    oc = []
    for j in range(REQ):
        scores = lax.dot_general(
            qall[j].reshape(NE * HD, QW), kcat[j], (((1,), (1,)), ((), ())), preferred_element_type=F32
        )
        scores = jnp.where(lanes < length_ref[0, j], scores * score_scale, HIDDEN_SCORE)
        highest = jnp.max(scores, axis=-1, keepdims=True)
        likely = jnp.exp(scores - highest)
        total = jnp.sum(likely, axis=-1, keepdims=True)
        out = jnp.dot(likely.astype(BF), kcat[j, :, :LAT], preferred_element_type=F32) / total
        tail = three_parts(highest + jnp.log(total), side)
        out = out.astype(BF).reshape(NY, 2, HD, LAT)
        tail = tail.reshape(NY, 2, HD, QW - LAT)
        for core in range(2):
            opart[core, j, :, :, :LAT] = out[:, core]
            opart[core, j, :, :, LAT:] = tail[:, core]
        oc.append(start(opart.at[1 - k, j], osib.at[j], os_s.at[j], os_r.at[j], sib))

    for copy in tc + gains:
        copy.wait_recv()
    squares = jnp.zeros((SLOTS, 1), F32)
    for g in range(NE):
        rows = tall[g].astype(F32)
        squares = squares + jnp.sum(rows * rows, axis=-1, keepdims=True)
    inverse = lax.rsqrt(squares / D + 1e-06)
    for g in range(NE):
        for b in range(FEAT // 128):
            part = tall[g, :, b * 128:(b + 1) * 128].astype(F32)
            xn[g, :, b * 128:(b + 1) * 128] = (part * inverse * gall[g, b:b + 1, :]).astype(BF)

    side = iota((NY * HD, QW - LAT), 1)
    for j in range(REQ):
        oc[j].wait_recv()
        values, level = merge([opart[k, j].reshape(NY * HD, QW), osib[j].reshape(NY * HD, QW)])
        omine[:, j, :, :LAT] = values.astype(BF).reshape(NY, HD, LAT)
        omine[:, j, :, LAT:] = three_parts(level, side).reshape(NY, HD, QW - LAT)
    oy = [
        start(omine.at[lax.rem(y + d, NY)], oin.at[d - 1], o_s.at[d - 1], o_r.at[d - 1], yp(d))
        for d in range(1, NY)
    ]

    for load in loads[1:]:
        load.wait()
    gate = jnp.zeros((SLOTS, FF), F32)
    up = jnp.zeros((SLOTS, FF), F32)
    for g in range(NE):
        gate = gate + jnp.dot(xn[g], wg[g * FEAT:(g + 1) * FEAT, :], preferred_element_type=F32)
        up = up + jnp.dot(xn[g], wu[g * FEAT:(g + 1) * FEAT, :], preferred_element_type=F32)
    hidden = (jax.nn.silu(gate) * up).astype(BF)

    def project(target):
        columns = pl.ds(pl.multiple_of(target * FEAT, BLK), FEAT)
        return jnp.dot(hidden, wd[:, columns], preferred_element_type=F32)

    yk = []
    for d in range(NY):
        ysib[d] = project(lax.rem(y + d + 1, NY) * 2 + 1 - k).astype(BF)
        yk.append(start(ysib.at[d], ysr.at[d], yk_s.at[d], yk_r.at[d], sib))
    yy = []
    for d in range(NY):
        yown[d] = project(lax.rem(y + d + 1, NY) * 2 + k)
    for d in range(NY - 1):
        yk[d].wait_recv()
        ysend[d] = (yown[d] + ysr[d].astype(F32)).astype(BF)
        yy.append(start(ysend.at[d], yrecv.at[d], yy_s.at[d], yy_r.at[d], yp(d + 1)))

    for copy in oy:
        copy.wait_recv()
    for j in range(REQ):
        values, level = merge([omine[y, j]] + [oin[d, j] for d in range(NY - 1)])
        og[z, j] = values.astype(BF)
    back = Gather(og, og_s, og_r, x, z, e)
    back.start()

    yk[NY - 1].wait_recv()
    summed = yown[NY - 1] + ysr[NY - 1].astype(F32)
    back.forward()
    for copy in yy:
        copy.wait_recv()
    for d in range(NY - 1):
        summed = summed + yrecv[d].astype(F32)
    rounded = summed.astype(BF)
    first_rows = (((0,), (0,)), ((), ()))
    both = lax.dot_general(phi[...], rounded, first_rows, preferred_element_type=F32)
    both = both + lax.dot_general(plo[...], rounded, first_rows, preferred_element_type=F32)
    tw[...] = both.reshape(NX, 32, FEAT)
    xr = []
    for d in range(1, NX):
        xrs[d - 1] = tw[lax.rem(x + d, NX)].astype(BF)
        xr.append(start(xrs.at[d - 1], xrr.at[d - 1], xr_s.at[d - 1], xr_r.at[d - 1], xp(d)))
    for copy in xr:
        copy.wait_recv()
    own = tw[x]
    for d in range(NX - 1):
        own = own + xrr[d].astype(F32)
    for t in range(NZ):
        zs[t, 0:4, 0:512] = own[4 * t:4 * t + 4, 0:512]
        zs[t, 4:8, 0:384] = own[4 * t:4 * t + 4, 512:896]
        zs[t, 4:8, 384:512] = jnp.zeros((4, 128), F32)
    zc = [
        start(zs.at[lax.rem(z + d, NZ)], zr.at[d - 1], zr_s.at[d - 1], zr_r.at[d - 1], zp(d)) for d in around
    ]

    back.finish()
    ox = []
    for d in range(1, NX):
        target = lax.rem(x + d, NX)
        for j in range(REQ):
            r = table[2, (target * NZ + z) * REQ + j]
            oxs[d - 1, j] = og[bits(r, 2, NZ), bits(r, 0, REQ)]
        ox.append(start(oxs.at[d - 1], oxr.at[x], ox_s.at[d - 1], ox_r.at[d - 1], xp(d)))
    for j in range(REQ):
        r = table[2, c * REQ + j]
        oxr[x, j] = og[bits(r, 2, NZ), bits(r, 0, REQ)]

    for copy in zc:
        copy.wait_recv()
    final = zs[z]
    for d in range(NZ - 1):
        final = final + zr[d]
    moe_ref[:, 0:512] = final[0:4, :].astype(BF)
    moe_ref[:, 512:896] = final[4:8, 0:384].astype(BF)

    for copy in ox:
        copy.wait_recv()
    for j in range(REQ):
        values = oxr[bits(table[2, c * REQ + j], 5, NX), j].astype(F32)
        for h in range(HD):
            af[j:j + 1, h * LAT:(h + 1) * LAT] = values[h:h + 1, :]
    att_ref[...] = af[...].astype(BF)
    for copy in pending:
        copy.wait_send()
    gather.drain()
    back.drain()


def layer(owner, lengths, routes, combine, q, qr, tok, gain, rope, lat, wg, wu, wd):
    vmem = pl.BlockSpec(memory_space=pltpu.VMEM)
    smem = pl.BlockSpec(memory_space=pltpu.SMEM)
    hbm = pl.BlockSpec(memory_space=pl.ANY)
    dma = pltpu.SemaphoreType.DMA
    V = pltpu.VMEM
    pairs = []
    for count in (7, 7, 7, 3, 3, 3, 7, 14, 3, 3, 4, 3, 4, 4, 3, 4, 3, 3, 7, 14, 3):
        pairs += [dma((count,)), dma((count,))]
    return pl.pallas_call(
        layer_kernel,
        out_shape=(
            jax.ShapeDtypeStruct((REQ, HD * LAT), BF),
            jax.ShapeDtypeStruct((REQ, FEAT), BF),
        ),
        in_specs=[smem] * 4 + [vmem] * 5 + [hbm] * 4,
        out_specs=(vmem, vmem),
        scratch_shapes=[
            pltpu.SMEM((8, 128), jnp.int32),
            V((D, FF), BF), V((D, FF), BF), V((FF, D), BF),
            V((REQ, POS, LAT), BF), V((REQ, POS, QW), BF),
            V((NZ, REQ, HD, QW), BF),
            V((NX, REQ, HD, QW), BF), V((NX - 1, REQ, HD, QW), BF),
            V((REQ, NE, HD, QW), BF),
            V((SLOTS, FEAT), BF), V((NE, SLOTS, FEAT), BF), V((NE, SLOTS, FEAT), BF),
            V((2, REQ, NY, HD, QW), BF), V((REQ, NY, HD, QW), BF),
            V((NY, REQ, HD, QW), BF), V((NY - 1, REQ, HD, QW), BF),
            V((NY, SLOTS, FEAT), BF), V((NY, SLOTS, FEAT), BF), V((NY, SLOTS, FEAT), F32),
            V((NY - 1, SLOTS, FEAT), BF), V((NY - 1, SLOTS, FEAT), BF),
            V((NX, 32, FEAT), F32),
            V((NX - 1, 32, FEAT), BF), V((NX - 1, 32, FEAT), BF),
            V((NZ, 8, 512), F32), V((NZ - 1, 8, 512), F32),
            V((NZ, REQ, HD, LAT), BF),
            V((NX - 1, REQ, HD, LAT), BF), V((NX, REQ, HD, LAT), BF),
            V((REQ, HD * LAT), F32),
            V((16, 256), F32), V((16, 256), BF), V((NX, NZ, 16, 256), BF),
            V((NE, 7, 128), F32),
            V((NZ, 8, 128), F32), V((NZ, 8, 128), F32),
            V((8, 128), F32), V((NX, 8, 128), F32), V((8, 128), F32),
            V((NZ, 8, 128), jnp.int32), V((NX, 8, 128), jnp.int32), V((8, 128), jnp.int32),
            V((SLOTS, 128), BF), V((SLOTS, 128), BF),
            dma((4,)), dma((1,)),
        ] + pairs,
        compiler_params=pltpu.CompilerParams(
            collective_id=0, has_side_effects=True, vmem_limit_bytes=48 * 1024 * 1024
        ),
    )(owner, lengths, routes, combine, q, qr, tok, gain, rope, lat, wg, wu, wd)


def local(
    latent_plane,
    latent_rope,
    query_plane,
    query_rope,
    decode_hidden,
    lengths,
    owner,
    norm_gain,
    routes,
    combine,
    gate_weight,
    up_weight,
    down_weight,
):
    rope = jnp.pad(latent_rope.reshape(REQ, POS, ROPE), ((0, 0), (0, 0), (0, QW - LAT - ROPE)))
    return layer(
        owner, lengths, routes, combine, query_plane, query_rope, decode_hidden,
        norm_gain.reshape(7, 128), rope, latent_plane, gate_weight, up_weight, down_weight,
    )


def solution(mesh):
    placed = (
        P("ctx", "expert", None),
        P("ctx", "expert"),
        P("ctx", "expert", None),
        P("ctx", "expert"),
        P("ctx", "expert"),
        P("ctx", None),
        P("ctx", None),
        P("expert"),
        P("ctx", None),
        P("ctx", None),
        P("ctx", None, "expert"),
        P("ctx", None, "expert"),
        P("ctx", "expert", None),
    )
    return jax.shard_map(
        local,
        mesh=mesh,
        in_specs=placed,
        out_specs=(P("ctx", "expert"), P("ctx", "expert")),
        check_vma=False,
    )
```

```python
import functools

import jax
import jax.numpy as jnp
from jax import lax
from jax.experimental import pallas as pl
from jax.experimental.pallas import tpu as pltpu
from jax.sharding import PartitionSpec as P

D = 7168
LAT = 512
ROPE = 64
BLK = 128
NX = 4
NZ = 8
NE = 8
NY = 4
REQ = 4
HD = 16
QW = 640
POS = 256
CAP = 3
SLOTS = NX * NZ * CAP
SENDS = 48
RECVS = 57
FEAT = D // NE
FF = 256

MESH = pl.DeviceIdType.MESH
BF = jnp.bfloat16
F32 = jnp.float32
score_scale = 192.0 ** (-0.5)
pack_limit = 448.0
HIDDEN_SCORE = -1e30


def coordinates():
    c = lax.axis_index("ctx")
    e = lax.axis_index("expert")
    return c, e, lax.div(c, NZ), lax.rem(c, NZ), lax.div(e, 2), lax.rem(e, 2)


def greet(peers):
    barrier = pltpu.get_barrier_semaphore()
    for peer in peers:
        pl.semaphore_signal(barrier, inc=1, device_id=peer, device_id_type=MESH)
    return lambda: pl.semaphore_wait(barrier, len(peers))


def remote(src, dst, send_sem, recv_sem, peer):
    return pltpu.make_async_remote_copy(
        src_ref=src,
        dst_ref=dst,
        send_sem=send_sem,
        recv_sem=recv_sem,
        device_id=peer,
        device_id_type=MESH,
    )


class Gather:
    def __init__(self, buf, start, sems, x, z, e):
        self.buf, self.start_copy, self.sems = buf, start, sems
        self.x, self.z, self.e = x, z, e
        self.second = {}

    def put(self, origin, hop, sign, low):
        block = self.buf.at[lax.rem(self.z + 2 * NZ - sign * origin, NZ), pl.ds(low, 2)]
        peer = (self.x * NZ + lax.rem(self.z + 2 * NZ + sign * hop, NZ), self.e)
        if origin + hop == 2:
            sem = self.sems[len(self.second)]
            self.second[sign, low] = self.start_copy(block, block, sem, peer)
        else:
            self.start_copy(block, block, self.sems[4], peer)

    def start(self, lows=(0, 2)):
        for hop in (2, 1):
            for low in lows:
                for sign in (1, -1):
                    self.put(0, hop, sign, low)

    def forward(self):
        for first in (True, False):
            for sign in (1, -1):
                low = 0 if first == (sign == 1) else 2
                self.second[sign, low].wait_recv()
                if first:
                    self.put(2, 2, sign, low)
                self.put(2, 1, sign, low)

    def finish(self):
        arrived(self.sems[4], self.buf.at[pl.ds(0, 5)])


def arrived(sem, blocks):
    pltpu.make_async_copy(blocks, blocks, sem).wait()


def three_parts(level, side):
    first = level.astype(BF).astype(F32)
    second = (level - first).astype(BF).astype(F32)
    third = level - first - second
    return jnp.where(side == 0, first, jnp.where(side == 1, second, jnp.where(side == 2, third, 0.0))).astype(BF)


def merge(parts):
    levels = [jnp.sum(part[:, LAT:].astype(F32), axis=-1, keepdims=True) for part in parts]
    top = functools.reduce(jnp.maximum, levels)
    share = [jnp.exp(level - top) for level in levels]
    total = functools.reduce(jnp.add, share)
    acc = share[0] * parts[0][:, :LAT].astype(F32)
    for weight, part in zip(share[1:], parts[1:]):
        acc = acc + weight * part[:, :LAT].astype(F32)
    return acc / total, top + jnp.log(total)


def bits(number, shift, count):
    return jnp.bitwise_and(jnp.right_shift(number, shift), count - 1)


def iota(shape, axis):
    return lax.broadcasted_iota(jnp.int32, shape, axis)


def layer_kernel(
    owner_hbm, length_hbm, routes_hbm, combine_hbm,
    q_hbm, qr_hbm, tok_hbm, gain_hbm, rope_hbm,
    lat_hbm, wg_hbm, wu_hbm, wd_hbm,
    att_hbm, moe_hbm,
    att_ref, moe_ref, owner_ref, length_ref, routes_ref, combine_ref, qr_ref, tok_ref, gain_ref, rope_ref, ropef, table, wg, wu, wd, lat, kcat, qz, xbuf0, xbuf1, xbuf2, xbuf3, xsend, qall, xt, tall, xn, opart, osib, omine, oin,
    ysib, ysr, yown, ysend, yrecv, tw, xrs, xrr, zs, zr, og, oxs, oxr,
    tokf, tokb, tk, gall, mzs, mzr, mxs, mxr, mrow, owz, owx, tbl, phi, plo,
    w_sem, s_sem, t_sem, out_sem, send_sems, recv_sems,
):
    c, e, x, z, y, k = coordinates()
    pending = []
    xbuf = (xbuf0, xbuf1, xbuf2, xbuf3)

    def zp(d):
        return (x * NZ + lax.rem(z + d, NZ), e)

    def xp(d):
        return (lax.rem(x + d, NX) * NZ + z, e)

    def ep(d):
        return (c, lax.rem(e + d, NE))

    def yp(d):
        return (c, lax.rem(y + d, NY) * 2 + k)

    sib = (c, y * 2 + 1 - k)

    def start(src, dst, recv_sem, peer):
        n = len(pending)
        if n >= SENDS:
            pending[n - SENDS].wait_send()
        copy = remote(src, dst, send_sems.at[n % SENDS], recv_sem, peer)
        copy.start()
        pending.append(copy)
        return copy

    taken = [0]

    def take(count):
        taken[0] += count
        return [recv_sems.at[taken[0] - count + n] for n in range(count)]

    oz_r, mz_r, kz_r, wx_r, mx_r, kx_r, g_r, tk_r, ox_r, yy_r, xr_r, zr_r = take(12)
    qx_r, qk_r, os_r, o_r, yk_r = (take(4) for _ in range(5))
    ty_r, qy_r, gather_r, back_r = take(3), take(12), take(5), take(5)

    loads = [
        pltpu.make_async_copy(lat_hbm, lat, w_sem.at[0]),
        pltpu.make_async_copy(wg_hbm.at[0], wg, w_sem.at[1]),
        pltpu.make_async_copy(wu_hbm.at[0], wu, w_sem.at[2]),
        pltpu.make_async_copy(wd_hbm.at[0], wd, w_sem.at[3]),
    ]
    blocks = (
        (routes_hbm, routes_ref), (combine_hbm, combine_ref), (owner_hbm, owner_ref), (length_hbm, length_ref),
        (qr_hbm, qr_ref), (q_hbm, qz.at[z, :, :, pl.ds(0, LAT)]), (tok_hbm, tok_ref), (gain_hbm, gain_ref),
        (rope_hbm, rope_ref),
    )
    small = [pltpu.make_async_copy(src, dst, s_sem.at[n]) for n, (src, dst) in enumerate(blocks)]
    for load in small:
        load.start()
    loads[0].start()
    wait_for_all = greet(
        [zp(d) for d in range(1, NZ)] + [xp(d) for d in range(1, NX)] + [ep(d) for d in range(1, NE)]
    )
    for load in loads[1:]:
        load.start()
    for load in small[:-1]:
        load.wait()

    lane = iota((8, 128), 1)
    mine = jnp.zeros((8, 128), jnp.int32)
    for j in range(REQ):
        mine = jnp.where(lane == c * REQ + j, owner_ref[0, j], mine)
    owz[z] = mine
    row = iota((64, 128), 0)
    expert = jnp.bitwise_and(row, 7) * NZ + jnp.right_shift(row, 3)
    wide = iota((64, 128), 1)
    weights = jnp.zeros((64, 128), F32)
    for j in range(REQ):
        for n in range(8):
            hit = (expert == routes_ref[j, n]) & (wide == c * REQ + j)
            weights = jnp.where(hit, combine_ref[j, n], weights)
    mzs[...] = weights.reshape(8, 8, 128)
    state = tok_ref[...].astype(F32)
    for g in range(4):
        width = 256 if g < 3 else 128
        tokf[4 * g:4 * g + 4, 0:width] = state[:, g * 256:g * 256 + width]
    tokf[12:16, 128:256] = jnp.zeros((4, 128), F32)
    tokb[...] = tokf[...].astype(BF)
    gall[e] = gain_ref[...]
    turned = jnp.concatenate(
        [
            jnp.where(
                jnp.right_shift(iota((HD, HD * ROPE), 1), 6) == iota((HD, HD * ROPE), 0),
                jnp.broadcast_to(qr_ref[...].astype(F32)[j:j + 1, :], (HD, HD * ROPE)),
                0.0,
            )
            for j in range(REQ)
        ],
        axis=0,
    ).astype(BF)
    fold = (jnp.bitwise_and(iota((HD * ROPE, 128), 0), 63) == iota((HD * ROPE, 128), 1)).astype(F32).astype(BF)
    qz[z, :, :, LAT:] = jnp.dot(turned, fold, preferred_element_type=F32).astype(BF).reshape(REQ, HD, 128)

    wait_for_all()
    around = (1, 7, 2, 6, 3, 5, 4)
    for d in around:
        start(owz.at[z], owz.at[z], oz_r, zp(d))
    for d in around:
        start(mzs.at[lax.rem(z + d, NZ)], mzr.at[z], mz_r, zp(d))
    for d in around:
        start(tokb, tk.at[x, z], kz_r, zp(d))
    gather = Gather(qz, start, gather_r, x, z, e)
    gather.start()
    for d in range(1, NE):
        start(gain_ref, gall.at[e], g_r, ep(d))
    mzr[z] = mzs[z]
    tk[x, z] = tokb[...]

    small[-1].wait()
    for t in range(POS // 2):
        ropef[:, t, :] = rope_ref[:, t * 128:(t + 1) * 128].astype(F32)
    position = iota((POS, POS // 2), 0)
    pair = iota((POS, POS // 2), 1) * 2
    even = (position == pair).astype(F32).astype(BF)
    odd = (position == pair + 1).astype(F32).astype(BF)
    low = iota((POS // 2, 128), 1) < ROPE
    for j in range(REQ):
        rows = ropef[j]
        near = jnp.where(low, rows, 0.0).astype(BF)
        far = jnp.where(low, pltpu.roll(rows, ROPE, 1), 0.0).astype(BF)
        turned = jnp.dot(even, near, preferred_element_type=F32) + jnp.dot(odd, far, preferred_element_type=F32)
        kcat[j, :, LAT:] = turned.astype(BF)

    loads[0].wait()
    for j in range(REQ):
        for b in range(LAT // BLK):
            block = lat[j, :, b * BLK:(b + 1) * BLK].astype(F32)
            scale = ((jnp.max(jnp.abs(block), axis=-1, keepdims=True) + 1e-06) / pack_limit).astype(BF)
            scale = scale.astype(F32)
            packed = (block / scale).astype(BF)
            kcat[j, :, b * BLK:(b + 1) * BLK] = (packed.astype(F32) * scale).astype(BF)

    arrived(oz_r, owz.at[pl.ds(0, NZ - 1)])
    arrived(mz_r, mzr.at[pl.ds(0, NZ - 1)])
    owx[x] = functools.reduce(jnp.add, [owz[d] for d in range(NZ)])
    mxs[...] = functools.reduce(jnp.add, [mzr[d] for d in range(NZ)])
    mxr[x] = mxs[...]
    for d in range(1, NX):
        start(owx.at[x], owx.at[x], wx_r, xp(d))
    for d in range(1, NX):
        start(mxs, mxr.at[x], mx_r, xp(d))
    arrived(kz_r, tk.at[0, pl.ds(0, NZ - 1)])
    for d in range(1, NX):
        start(tk.at[x], tk.at[x], kx_r, xp(d))
    gather.forward()

    arrived(wx_r, owx.at[pl.ds(0, NX - 1)])
    arrived(mx_r, mxr.at[pl.ds(0, NX - 1)])
    sub = iota((128, 128), 0)
    col = iota((128, 128), 1)
    owners = functools.reduce(jnp.add, [owx[d] for d in range(NX)])[0:1, :]
    across = jnp.broadcast_to(owners, (128, 128))
    rank = jnp.sum(jnp.where((across.T == across) & (sub < col), 1, 0), axis=0, keepdims=True)
    place = jnp.broadcast_to(owners * REQ + rank, (128, 128)).T
    request_of = jnp.sum(jnp.where(place == col, sub, 0), axis=0, keepdims=True)
    eight = iota((8, 128), 0)
    tbl[...] = jnp.where(eight == 0, owners, jnp.where(eight == 1, rank, request_of))
    to_scalars = pltpu.make_async_copy(tbl, table, t_sem.at[0])
    to_scalars.start()

    mrow[...] = functools.reduce(jnp.add, [mxr[d] for d in range(NX)])
    share = mrow[pl.ds(x, 1), :]
    chosen = jnp.where(share > 0, 1.0, 0.0)
    earlier = ((jnp.right_shift(sub, 2) == jnp.right_shift(col, 2)) & (sub < col)).astype(F32).astype(BF)
    before = jnp.dot(jnp.broadcast_to(chosen, (8, 128)).astype(BF), earlier, preferred_element_type=F32)[0:1, :]
    slot = (jnp.right_shift(iota((1, 128), 1), 2) * CAP).astype(F32) + before
    placing = jnp.where(iota((SLOTS, 128), 0).astype(F32) == slot, chosen, 0.0)
    scaled = placing * share
    high = scaled.astype(BF)
    phi[...] = high
    plo[...] = (scaled - high.astype(F32)).astype(BF)
    token_of = iota((128, 512), 1)
    token_of = jnp.right_shift(token_of, 4) * REQ + jnp.bitwise_and(token_of, 3)
    widen = (token_of == iota((128, 512), 0)).astype(F32).astype(BF)
    placing = jnp.dot(placing.astype(BF), widen, preferred_element_type=F32)
    group = jnp.bitwise_and(jnp.right_shift(iota((SLOTS, 512), 1), 2), 3)
    arrived(kx_r, tk.at[pl.ds(0, NX - 1)])
    states = tk[...].reshape(512, 256)
    for g in range(4):
        width = 256 if g < 3 else 128
        part = jnp.where(group == g, placing, 0.0).astype(BF)
        xt[:, g * 256:g * 256 + width] = jnp.dot(
            part, states[:, 0:width], preferred_element_type=F32
        ).astype(BF)

    ty = [start(xt, tall.at[e], ty_r[d - 1], yp(d)) for d in range(1, NY)]
    start(xt, tall.at[e], tk_r, sib)
    tall[e] = xt[...]

    gather.finish()
    to_scalars.wait()
    for j in range(REQ):
        for d in range(1, NX):
            r = (lax.rem(x + d, NX) * NZ + z) * REQ + j
            xsend[d - 1, j] = qz[bits(table[0, r], 0, NZ), bits(table[1, r], 0, REQ)]
            start(xsend.at[d - 1, j], xbuf[j].at[x], qx_r[j], xp(d))
        r = c * REQ + j
        xbuf[j][x] = qz[bits(table[0, r], 0, NZ), bits(table[1, r], 0, REQ)]

    qy = []
    for j in range(REQ):
        arrived(qx_r[j], xbuf[j].at[pl.ds(0, NX - 1)])
        qall[j, e] = xbuf[j][bits(table[0, c * REQ + j], 3, NX)]
        block = qall.at[j, e]
        for d in range(1, NY):
            qy.append(start(block, block, qy_r[j * 3 + d - 1], yp(d)))
        start(block, block, qk_r[j], sib)
    for d in range(1, NY):
        ty[d - 1].wait_recv()
        other = lax.rem(y + NY - d, NY) * 2 + k
        start(tall.at[other], tall.at[other], tk_r, sib)
    for j in range(REQ):
        for d in range(1, NY):
            qy[j * 3 + d - 1].wait_recv()
            block = qall.at[j, lax.rem(y + NY - d, NY) * 2 + k]
            start(block, block, qk_r[j], sib)

    lanes = iota((1, POS), 1) + e * POS
    side = iota((HD * NE, QW - LAT), 1)
    oc = []
    for j in range(REQ):
        arrived(qk_r[j], qall.at[j, pl.ds(0, NY)])
        scores = lax.dot_general(
            qall[j].reshape(NE * HD, QW), kcat[j], (((1,), (1,)), ((), ())), preferred_element_type=F32
        )
        scores = jnp.where(lanes < length_ref[0, j], scores * score_scale, HIDDEN_SCORE)
        highest = jnp.max(scores, axis=-1, keepdims=True)
        likely = jnp.exp(scores - highest)
        total = jnp.sum(likely, axis=-1, keepdims=True)
        out = jnp.dot(likely.astype(BF), kcat[j, :, :LAT], preferred_element_type=F32) / total
        tail = three_parts(highest + jnp.log(total), side)
        out = out.astype(BF).reshape(NY, 2, HD, LAT)
        tail = tail.reshape(NY, 2, HD, QW - LAT)
        for core in range(2):
            opart[core, j, :, :, :LAT] = out[:, core]
            opart[core, j, :, :, LAT:] = tail[:, core]
        oc.append(start(opart.at[1 - k, j], osib.at[j], os_r[j], sib))

    arrived(tk_r, tall.at[pl.ds(0, NY)])
    arrived(g_r, gall.at[pl.ds(0, NE - 1)])
    squares = jnp.zeros((SLOTS, 1), F32)
    for g in range(NE):
        rows = tall[g].astype(F32)
        squares = squares + jnp.sum(rows * rows, axis=-1, keepdims=True)
    inverse = lax.rsqrt(squares / D + 1e-06)
    for g in range(NE):
        for b in range(FEAT // 128):
            part = tall[g, :, b * 128:(b + 1) * 128].astype(F32)
            xn[g, :, b * 128:(b + 1) * 128] = (part * inverse * gall[g, b:b + 1, :]).astype(BF)

    side = iota((NY * HD, QW - LAT), 1)
    for j in range(REQ):
        oc[j].wait_recv()
        values, level = merge([opart[k, j].reshape(NY * HD, QW), osib[j].reshape(NY * HD, QW)])
        omine[:, j, :, :LAT] = values.astype(BF).reshape(NY, HD, LAT)
        omine[:, j, :, LAT:] = three_parts(level, side).reshape(NY, HD, QW - LAT)
        for d in range(1, NY):
            start(omine.at[lax.rem(y + d, NY), j], oin.at[d - 1, j], o_r[j], yp(d))

    for load in loads[1:]:
        load.wait()
    gate = jnp.zeros((SLOTS, FF), F32)
    up = jnp.zeros((SLOTS, FF), F32)
    for g in range(NE):
        gate = gate + jnp.dot(xn[g], wg[g * FEAT:(g + 1) * FEAT, :], preferred_element_type=F32)
        up = up + jnp.dot(xn[g], wu[g * FEAT:(g + 1) * FEAT, :], preferred_element_type=F32)
    hidden = (jax.nn.silu(gate) * up).astype(BF)

    def project(target):
        columns = pl.ds(pl.multiple_of(target * FEAT, BLK), FEAT)
        return jnp.dot(hidden, wd[:, columns], preferred_element_type=F32)

    yk = []
    for d in range(NY):
        ysib[d] = project(lax.rem(y + d + 1, NY) * 2 + 1 - k).astype(BF)
        yk.append(start(ysib.at[d], ysr.at[d], yk_r[d], sib))
    for d in range(NY):
        yown[d] = project(lax.rem(y + d + 1, NY) * 2 + k)
    for d in range(NY - 1):
        yk[d].wait_recv()
        ysend[d] = (yown[d] + ysr[d].astype(F32)).astype(BF)
        start(ysend.at[d], yrecv.at[d], yy_r, yp(d + 1))

    back = Gather(og, start, back_r, x, z, e)
    for j in range(REQ):
        arrived(o_r[j], oin.at[:, j])
        values, level = merge([omine[y, j]] + [oin[d, j] for d in range(NY - 1)])
        og[z, j] = values.astype(BF)
        if j % 2 == 1:
            back.start((j - 1,))

    yk[NY - 1].wait_recv()
    summed = yown[NY - 1] + ysr[NY - 1].astype(F32)
    back.forward()
    arrived(yy_r, yrecv)
    for d in range(NY - 1):
        summed = summed + yrecv[d].astype(F32)
    rounded = summed.astype(BF)
    first_rows = (((0,), (0,)), ((), ()))
    both = lax.dot_general(phi[...], rounded, first_rows, preferred_element_type=F32)
    both = both + lax.dot_general(plo[...], rounded, first_rows, preferred_element_type=F32)
    tw[...] = both.reshape(NX, 32, FEAT)
    for d in range(1, NX):
        xrs[d - 1] = tw[lax.rem(x + d, NX)].astype(BF)
        start(xrs.at[d - 1], xrr.at[d - 1], xr_r, xp(d))
    arrived(xr_r, xrr)
    own = tw[x]
    for d in range(NX - 1):
        own = own + xrr[d].astype(F32)
    for t in range(NZ):
        zs[t, 0:4, 0:512] = own[4 * t:4 * t + 4, 0:512]
        zs[t, 4:8, 0:384] = own[4 * t:4 * t + 4, 512:896]
        zs[t, 4:8, 384:512] = jnp.zeros((4, 128), F32)
    for d in around:
        start(zs.at[lax.rem(z + d, NZ)], zr.at[d - 1], zr_r, zp(d))

    back.finish()
    for d in range(1, NX):
        target = lax.rem(x + d, NX)
        for j in range(REQ):
            r = table[2, (target * NZ + z) * REQ + j]
            oxs[d - 1, j] = og[bits(r, 2, NZ), bits(r, 0, REQ)]
        start(oxs.at[d - 1], oxr.at[x], ox_r, xp(d))
    for j in range(REQ):
        r = table[2, c * REQ + j]
        oxr[x, j] = og[bits(r, 2, NZ), bits(r, 0, REQ)]

    arrived(zr_r, zr)
    final = zs[z]
    for d in range(NZ - 1):
        final = final + zr[d]
    moe_ref[:, 0:512] = final[0:4, :]
    moe_ref[:, 512:896] = final[4:8, 0:384]
    moe_out = pltpu.make_async_copy(moe_ref, moe_hbm, out_sem.at[0])
    moe_out.start()
    att_out = pltpu.make_async_copy(att_ref, att_hbm, out_sem.at[1])

    arrived(ox_r, oxr.at[pl.ds(0, NX - 1)])
    for j in range(REQ):
        values = oxr[bits(table[2, c * REQ + j], 5, NX), j].astype(F32)
        for h in range(HD):
            att_ref[j:j + 1, h * LAT:(h + 1) * LAT] = values[h:h + 1, :]
    att_out.start()
    for copy in pending[-SENDS:]:
        copy.wait_send()
    moe_out.wait()
    att_out.wait()


def layer(owner, lengths, routes, combine, q, qr, tok, gain, rope, lat, wg, wu, wd):
    hbm = pl.BlockSpec(memory_space=pltpu.HBM)
    dma = pltpu.SemaphoreType.DMA
    V = pltpu.VMEM
    return pl.pallas_call(
        layer_kernel,
        out_shape=(
            jax.ShapeDtypeStruct((REQ, HD * LAT), F32),
            jax.ShapeDtypeStruct((REQ, FEAT), F32),
        ),
        in_specs=[hbm] * 13,
        out_specs=(hbm, hbm),
        scratch_shapes=[
            V((REQ, HD * LAT), F32), V((REQ, FEAT), F32),
            pltpu.SMEM((1, REQ), jnp.int32), pltpu.SMEM((1, REQ), jnp.int32),
            pltpu.SMEM((REQ, 8), jnp.int32), pltpu.SMEM((REQ, 8), F32),
            V((REQ, HD * ROPE), BF), V((REQ, FEAT), BF), V((7, 128), F32), V((REQ, POS * ROPE), BF), V((REQ, POS // 2, 128), F32),
            pltpu.SMEM((8, 128), jnp.int32),
            V((D, FF), BF), V((D, FF), BF), V((FF, D), BF),
            V((REQ, POS, LAT), BF), V((REQ, POS, QW), BF),
            V((NZ, REQ, HD, QW), BF),
            V((NX, HD, QW), BF), V((NX, HD, QW), BF), V((NX, HD, QW), BF), V((NX, HD, QW), BF),
            V((NX - 1, REQ, HD, QW), BF),
            V((REQ, NE, HD, QW), BF),
            V((SLOTS, FEAT), BF), V((NE, SLOTS, FEAT), BF), V((NE, SLOTS, FEAT), BF),
            V((2, REQ, NY, HD, QW), BF), V((REQ, NY, HD, QW), BF),
            V((NY, REQ, HD, QW), BF), V((NY - 1, REQ, HD, QW), BF),
            V((NY, SLOTS, FEAT), BF), V((NY, SLOTS, FEAT), BF), V((NY, SLOTS, FEAT), F32),
            V((NY - 1, SLOTS, FEAT), BF), V((NY - 1, SLOTS, FEAT), BF),
            V((NX, 32, FEAT), F32),
            V((NX - 1, 32, FEAT), BF), V((NX - 1, 32, FEAT), BF),
            V((NZ, 8, 512), F32), V((NZ - 1, 8, 512), F32),
            V((NZ, REQ, HD, LAT), BF),
            V((NX - 1, REQ, HD, LAT), BF), V((NX, REQ, HD, LAT), BF),
            V((16, 256), F32), V((16, 256), BF), V((NX, NZ, 16, 256), BF),
            V((NE, 7, 128), F32),
            V((NZ, 8, 128), F32), V((NZ, 8, 128), F32),
            V((8, 128), F32), V((NX, 8, 128), F32), V((8, 128), F32),
            V((NZ, 8, 128), jnp.int32), V((NX, 8, 128), jnp.int32), V((8, 128), jnp.int32),
            V((SLOTS, 128), BF), V((SLOTS, 128), BF),
            dma((4,)), dma((9,)), dma((1,)), dma((2,)), dma((SENDS,)), dma((RECVS,)),
        ],
        compiler_params=pltpu.CompilerParams(
            collective_id=0, has_side_effects=True, vmem_limit_bytes=64 * 1024 * 1024
        ),
    )(owner, lengths, routes, combine, q, qr, tok, gain, rope, lat, wg, wu, wd)


def local(
    latent_plane,
    latent_rope,
    query_plane,
    query_rope,
    decode_hidden,
    lengths,
    owner,
    norm_gain,
    routes,
    combine,
    gate_weight,
    up_weight,
    down_weight,
):
    attended, summed = layer(
        owner, lengths, routes, combine, query_plane, query_rope, decode_hidden,
        norm_gain.reshape(7, 128), latent_rope, latent_plane, gate_weight, up_weight, down_weight,
    )
    return attended.astype(BF), summed.astype(BF)


def solution(mesh):
    placed = (
        P("ctx", "expert", None),
        P("ctx", "expert"),
        P("ctx", "expert", None),
        P("ctx", "expert"),
        P("ctx", "expert"),
        P("ctx", None),
        P("ctx", None),
        P("expert"),
        P("ctx", None),
        P("ctx", None),
        P("ctx", None, "expert"),
        P("ctx", None, "expert"),
        P("ctx", "expert", None),
    )
    return jax.shard_map(
        local,
        mesh=mesh,
        in_specs=placed,
        out_specs=(P("ctx", "expert"), P("ctx", "expert")),
        check_vma=False,
    )
```

```python
import functools

import jax
import jax.numpy as jnp
from jax import lax
from jax.experimental import pallas as pl
from jax.experimental.pallas import tpu as pltpu
from jax.sharding import PartitionSpec as P

D = 7168
LAT = 512
ROPE = 64
BLK = 128
NX = 4
NZ = 8
NE = 8
NY = 4
REQ = 4
HD = 16
QW = 640
POS = 256
CAP = 3
SLOTS = NX * NZ * CAP
SENDS = 48
RECVS = 69
HALVES = ((0, 512), (512, 384))
FEAT = D // NE
FF = 256

MESH = pl.DeviceIdType.MESH
BF = jnp.bfloat16
F32 = jnp.float32
score_scale = 192.0 ** (-0.5)
pack_limit = 448.0
HIDDEN_SCORE = -1e30


def coordinates():
    c = lax.axis_index("ctx")
    e = lax.axis_index("expert")
    return c, e, lax.div(c, NZ), lax.rem(c, NZ), lax.div(e, 2), lax.rem(e, 2)


def greet(peers):
    barrier = pltpu.get_barrier_semaphore()
    for peer in peers:
        pl.semaphore_signal(barrier, inc=1, device_id=peer, device_id_type=MESH)
    return lambda: pl.semaphore_wait(barrier, len(peers))


def remote(src, dst, send_sem, recv_sem, peer):
    return pltpu.make_async_remote_copy(
        src_ref=src,
        dst_ref=dst,
        send_sem=send_sem,
        recv_sem=recv_sem,
        device_id=peer,
        device_id_type=MESH,
    )


class Gather:
    def __init__(self, buf, start, sems, x, z, e):
        self.buf, self.start_copy, self.sems = buf, start, sems
        self.x, self.z, self.e = x, z, e
        self.second = {}

    def put(self, origin, hop, sign, low):
        block = self.buf.at[lax.rem(self.z + 2 * NZ - sign * origin, NZ), pl.ds(low, 2)]
        peer = (self.x * NZ + lax.rem(self.z + 2 * NZ + sign * hop, NZ), self.e)
        if origin + hop == 2:
            sem = self.sems[len(self.second)]
            self.second[sign, low] = self.start_copy(block, block, sem, peer)
        else:
            self.start_copy(block, block, self.sems[4], peer)

    def start(self, lows=(0, 2)):
        for hop in (2, 1):
            for low in lows:
                for sign in (1, -1):
                    self.put(0, hop, sign, low)

    def forward(self):
        for first in (True, False):
            for sign in (1, -1):
                low = 0 if first == (sign == 1) else 2
                self.second[sign, low].wait_recv()
                if first:
                    self.put(2, 2, sign, low)
                self.put(2, 1, sign, low)

    def finish(self):
        arrived(self.sems[4], self.buf.at[pl.ds(0, 5)])


def arrived(sem, blocks):
    pltpu.make_async_copy(blocks, blocks, sem).wait()


def three_parts(level, side):
    first = level.astype(BF).astype(F32)
    second = (level - first).astype(BF).astype(F32)
    third = level - first - second
    return jnp.where(side == 0, first, jnp.where(side == 1, second, jnp.where(side == 2, third, 0.0))).astype(BF)


def merge(parts):
    levels = [jnp.sum(part[:, LAT:].astype(F32), axis=-1, keepdims=True) for part in parts]
    top = functools.reduce(jnp.maximum, levels)
    share = [jnp.exp(level - top) for level in levels]
    total = functools.reduce(jnp.add, share)
    acc = share[0] * parts[0][:, :LAT].astype(F32)
    for weight, part in zip(share[1:], parts[1:]):
        acc = acc + weight * part[:, :LAT].astype(F32)
    return acc / total, top + jnp.log(total)


def bits(number, shift, count):
    return jnp.bitwise_and(jnp.right_shift(number, shift), count - 1)


def iota(shape, axis):
    return lax.broadcasted_iota(jnp.int32, shape, axis)


def layer_kernel(
    owner_hbm, length_hbm, routes_hbm, combine_hbm,
    q_hbm, qr_hbm, tok_hbm, gain_hbm, rope_hbm,
    lat_hbm, wg_hbm, wu_hbm, wd_hbm,
    att_hbm, moe_hbm,
    af, att_ref, moe_ref, owner_ref, length_ref, routes_ref, combine_ref, qr_ref, tok_ref, gain_ref, rope_ref, ropef, table, wg, wu, wd, lat, kcat, qz, xbuf0, xbuf1, xbuf2, xbuf3, xsend, qall, xt, tall, xn, opart, osib, omine, oin,
    ysib, ysr, yown, ysend, yrecv, tw, xrs, xrr, zs, zr, og, oxs, oxr,
    tokf, tokb, tk, gall, mzs, mzr, mxs, mxr, mrow, owz, owx, tbl, phi, plo,
    w_sem, s_sem, t_sem, out_sem, send_sems, recv_sems,
):
    c, e, x, z, y, k = coordinates()
    pending = []
    xbuf = (xbuf0, xbuf1, xbuf2, xbuf3)

    def zp(d):
        return (x * NZ + lax.rem(z + d, NZ), e)

    def xp(d):
        return (lax.rem(x + d, NX) * NZ + z, e)

    def ep(d):
        return (c, lax.rem(e + d, NE))

    def yp(d):
        return (c, lax.rem(y + d, NY) * 2 + k)

    sib = (c, y * 2 + 1 - k)

    def start(src, dst, recv_sem, peer):
        n = len(pending)
        if n >= SENDS:
            pending[n - SENDS].wait_send()
        copy = remote(src, dst, send_sems.at[n % SENDS], recv_sem, peer)
        copy.start()
        pending.append(copy)
        return copy

    taken = [0]

    def take(count):
        taken[0] += count
        return [recv_sems.at[taken[0] - count + n] for n in range(count)]

    oz_r, mz_r, kz_r, wx_r, mx_r, kx_r, g_r, tk_r, ox_r = take(9)
    yy_r, xr_r, zr_r = take(2), take(2), take(2)
    qx_r, qk_r, os_r, o_r, yk_r = (take(4) for _ in range(5))
    ty_r, qy_r, gather_r, back_r = take(12), take(12), take(5), take(5)

    loads = [
        pltpu.make_async_copy(lat_hbm, lat, w_sem.at[0]),
        pltpu.make_async_copy(wg_hbm.at[0], wg, w_sem.at[1]),
        pltpu.make_async_copy(wu_hbm.at[0], wu, w_sem.at[2]),
        pltpu.make_async_copy(wd_hbm.at[0], wd, w_sem.at[3]),
    ]
    blocks = (
        (routes_hbm, routes_ref), (combine_hbm, combine_ref), (owner_hbm, owner_ref), (length_hbm, length_ref),
        (qr_hbm, qr_ref), (q_hbm, qz.at[z, :, :, pl.ds(0, LAT)]), (tok_hbm, tok_ref), (gain_hbm, gain_ref),
        (rope_hbm, rope_ref),
    )
    small = [pltpu.make_async_copy(src, dst, s_sem.at[n]) for n, (src, dst) in enumerate(blocks)]
    for load in small:
        load.start()
    loads[0].start()
    wait_for_all = greet(
        [zp(d) for d in range(1, NZ)] + [xp(d) for d in range(1, NX)] + [ep(d) for d in range(1, NE)]
    )
    for load in loads[1:]:
        load.start()
    for load in small[:-1]:
        load.wait()

    lane = iota((8, 128), 1)
    mine = jnp.zeros((8, 128), jnp.int32)
    for j in range(REQ):
        mine = jnp.where(lane == c * REQ + j, owner_ref[0, j], mine)
    owz[z] = mine
    row = iota((64, 128), 0)
    expert = jnp.bitwise_and(row, 7) * NZ + jnp.right_shift(row, 3)
    wide = iota((64, 128), 1)
    weights = jnp.zeros((64, 128), F32)
    for j in range(REQ):
        for n in range(8):
            hit = (expert == routes_ref[j, n]) & (wide == c * REQ + j)
            weights = jnp.where(hit, combine_ref[j, n], weights)
    mzs[...] = weights.reshape(8, 8, 128)
    state = tok_ref[...].astype(F32)
    for g in range(4):
        width = 256 if g < 3 else 128
        tokf[4 * g:4 * g + 4, 0:width] = state[:, g * 256:g * 256 + width]
    tokf[12:16, 128:256] = jnp.zeros((4, 128), F32)
    tokb[...] = tokf[...].astype(BF)
    gall[e] = gain_ref[...]
    turned = jnp.concatenate(
        [
            jnp.where(
                jnp.right_shift(iota((HD, HD * ROPE), 1), 6) == iota((HD, HD * ROPE), 0),
                jnp.broadcast_to(qr_ref[...].astype(F32)[j:j + 1, :], (HD, HD * ROPE)),
                0.0,
            )
            for j in range(REQ)
        ],
        axis=0,
    ).astype(BF)
    fold = (jnp.bitwise_and(iota((HD * ROPE, 128), 0), 63) == iota((HD * ROPE, 128), 1)).astype(F32).astype(BF)
    qz[z, :, :, LAT:] = jnp.dot(turned, fold, preferred_element_type=F32).astype(BF).reshape(REQ, HD, 128)

    wait_for_all()
    around = (1, 7, 2, 6, 3, 5, 4)
    for d in around:
        start(owz.at[z], owz.at[z], oz_r, zp(d))
    for d in around:
        start(mzs.at[lax.rem(z + d, NZ)], mzr.at[z], mz_r, zp(d))
    for d in around:
        start(tokb, tk.at[x, z], kz_r, zp(d))
    gather = Gather(qz, start, gather_r, x, z, e)
    gather.start()
    for d in range(1, NE):
        start(gain_ref, gall.at[e], g_r, ep(d))
    mzr[z] = mzs[z]
    tk[x, z] = tokb[...]

    small[-1].wait()
    for t in range(POS // 2):
        ropef[:, t, :] = rope_ref[:, t * 128:(t + 1) * 128].astype(F32)
    position = iota((POS, POS // 2), 0)
    pair = iota((POS, POS // 2), 1) * 2
    even = (position == pair).astype(F32).astype(BF)
    odd = (position == pair + 1).astype(F32).astype(BF)
    low = iota((POS // 2, 128), 1) < ROPE
    for j in range(REQ):
        rows = ropef[j]
        near = jnp.where(low, rows, 0.0).astype(BF)
        far = jnp.where(low, pltpu.roll(rows, ROPE, 1), 0.0).astype(BF)
        turned = jnp.dot(even, near, preferred_element_type=F32) + jnp.dot(odd, far, preferred_element_type=F32)
        kcat[j, :, LAT:] = turned.astype(BF)

    loads[0].wait()
    for j in range(REQ):
        for b in range(LAT // BLK):
            block = lat[j, :, b * BLK:(b + 1) * BLK].astype(F32)
            scale = ((jnp.max(jnp.abs(block), axis=-1, keepdims=True) + 1e-06) / pack_limit).astype(BF)
            scale = scale.astype(F32)
            packed = (block / scale).astype(BF)
            kcat[j, :, b * BLK:(b + 1) * BLK] = (packed.astype(F32) * scale).astype(BF)

    arrived(oz_r, owz.at[pl.ds(0, NZ - 1)])
    arrived(mz_r, mzr.at[pl.ds(0, NZ - 1)])
    owx[x] = functools.reduce(jnp.add, [owz[d] for d in range(NZ)])
    mxs[...] = functools.reduce(jnp.add, [mzr[d] for d in range(NZ)])
    mxr[x] = mxs[...]
    for d in range(1, NX):
        start(owx.at[x], owx.at[x], wx_r, xp(d))
    for d in range(1, NX):
        start(mxs, mxr.at[x], mx_r, xp(d))
    arrived(kz_r, tk.at[0, pl.ds(0, NZ - 1)])
    for d in range(1, NX):
        start(tk.at[x], tk.at[x], kx_r, xp(d))
    gather.forward()

    arrived(wx_r, owx.at[pl.ds(0, NX - 1)])
    arrived(mx_r, mxr.at[pl.ds(0, NX - 1)])
    sub = iota((128, 128), 0)
    col = iota((128, 128), 1)
    owners = functools.reduce(jnp.add, [owx[d] for d in range(NX)])[0:1, :]
    across = jnp.broadcast_to(owners, (128, 128))
    rank = jnp.sum(jnp.where((across.T == across) & (sub < col), 1, 0), axis=0, keepdims=True)
    place = jnp.broadcast_to(owners * REQ + rank, (128, 128)).T
    request_of = jnp.sum(jnp.where(place == col, sub, 0), axis=0, keepdims=True)
    eight = iota((8, 128), 0)
    tbl[...] = jnp.where(eight == 0, owners, jnp.where(eight == 1, rank, request_of))
    to_scalars = pltpu.make_async_copy(tbl, table, t_sem.at[0])
    to_scalars.start()

    mrow[...] = functools.reduce(jnp.add, [mxr[d] for d in range(NX)])
    share = mrow[pl.ds(x, 1), :]
    chosen = jnp.where(share > 0, 1.0, 0.0)
    earlier = ((jnp.right_shift(sub, 2) == jnp.right_shift(col, 2)) & (sub < col)).astype(F32).astype(BF)
    before = jnp.dot(jnp.broadcast_to(chosen, (8, 128)).astype(BF), earlier, preferred_element_type=F32)[0:1, :]
    slot = (jnp.right_shift(iota((1, 128), 1), 2) * CAP).astype(F32) + before
    placing = jnp.where(iota((SLOTS, 128), 0).astype(F32) == slot, chosen, 0.0)
    scaled = placing * share
    high = scaled.astype(BF)
    phi[...] = high
    plo[...] = (scaled - high.astype(F32)).astype(BF)
    token_of = iota((128, 512), 1)
    token_of = jnp.right_shift(token_of, 4) * REQ + jnp.bitwise_and(token_of, 3)
    widen = (token_of == iota((128, 512), 0)).astype(F32).astype(BF)
    placing = jnp.dot(placing.astype(BF), widen, preferred_element_type=F32)
    group = jnp.bitwise_and(jnp.right_shift(iota((SLOTS, 512), 1), 2), 3)
    arrived(kx_r, tk.at[pl.ds(0, NX - 1)])
    states = tk[...].reshape(512, 256)
    ty = []
    for g in range(4):
        width = 256 if g < 3 else 128
        part = jnp.where(group == g, placing, 0.0).astype(BF)
        columns = pl.ds(g * 256, width)
        xt[:, g * 256:g * 256 + width] = jnp.dot(
            part, states[:, 0:width], preferred_element_type=F32
        ).astype(BF)
        for d in range(1, NY):
            ty.append(start(xt.at[:, columns], tall.at[e, :, columns], ty_r[g * 3 + d - 1], yp(d)))
        start(xt.at[:, columns], tall.at[e, :, columns], tk_r, sib)

    tall[e] = xt[...]

    gather.finish()
    to_scalars.wait()
    for j in range(REQ):
        for d in range(1, NX):
            r = (lax.rem(x + d, NX) * NZ + z) * REQ + j
            xsend[d - 1, j] = qz[bits(table[0, r], 0, NZ), bits(table[1, r], 0, REQ)]
            start(xsend.at[d - 1, j], xbuf[j].at[x], qx_r[j], xp(d))
        r = c * REQ + j
        xbuf[j][x] = qz[bits(table[0, r], 0, NZ), bits(table[1, r], 0, REQ)]

    qy = []
    for j in range(REQ):
        arrived(qx_r[j], xbuf[j].at[pl.ds(0, NX - 1)])
        qall[j, e] = xbuf[j][bits(table[0, c * REQ + j], 3, NX)]
        block = qall.at[j, e]
        for d in range(1, NY):
            qy.append(start(block, block, qy_r[j * 3 + d - 1], yp(d)))
        start(block, block, qk_r[j], sib)
    for g in range(4):
        for d in range(1, NY):
            ty[g * 3 + d - 1].wait_recv()
            other = lax.rem(y + NY - d, NY) * 2 + k
            block = tall.at[other, :, pl.ds(g * 256, 256 if g < 3 else 128)]
            start(block, block, tk_r, sib)
    for j in range(REQ):
        for d in range(1, NY):
            qy[j * 3 + d - 1].wait_recv()
            block = qall.at[j, lax.rem(y + NY - d, NY) * 2 + k]
            start(block, block, qk_r[j], sib)

    lanes = iota((1, POS), 1) + e * POS
    side = iota((HD * NE, QW - LAT), 1)
    oc = []
    for j in range(REQ):
        arrived(qk_r[j], qall.at[j, pl.ds(0, NY)])
        scores = lax.dot_general(
            qall[j].reshape(NE * HD, QW), kcat[j], (((1,), (1,)), ((), ())), preferred_element_type=F32
        )
        scores = jnp.where(lanes < length_ref[0, j], scores * score_scale, HIDDEN_SCORE)
        highest = jnp.max(scores, axis=-1, keepdims=True)
        likely = jnp.exp(scores - highest)
        total = jnp.sum(likely, axis=-1, keepdims=True)
        out = jnp.dot(likely.astype(BF), kcat[j, :, :LAT], preferred_element_type=F32) / total
        tail = three_parts(highest + jnp.log(total), side)
        out = out.astype(BF).reshape(NY, 2, HD, LAT)
        tail = tail.reshape(NY, 2, HD, QW - LAT)
        for core in range(2):
            opart[core, j, :, :, :LAT] = out[:, core]
            opart[core, j, :, :, LAT:] = tail[:, core]
        oc.append(start(opart.at[1 - k, j], osib.at[j], os_r[j], sib))

    arrived(tk_r, tall.at[pl.ds(0, NY)])
    arrived(g_r, gall.at[pl.ds(0, NE - 1)])
    squares = jnp.zeros((SLOTS, 1), F32)
    for g in range(NE):
        rows = tall[g].astype(F32)
        squares = squares + jnp.sum(rows * rows, axis=-1, keepdims=True)
    inverse = lax.rsqrt(squares / D + 1e-06)
    for g in range(NE):
        for b in range(FEAT // 128):
            part = tall[g, :, b * 128:(b + 1) * 128].astype(F32)
            xn[g, :, b * 128:(b + 1) * 128] = (part * inverse * gall[g, b:b + 1, :]).astype(BF)

    side = iota((NY * HD, QW - LAT), 1)
    for j in range(REQ):
        oc[j].wait_recv()
        values, level = merge([opart[k, j].reshape(NY * HD, QW), osib[j].reshape(NY * HD, QW)])
        omine[:, j, :, :LAT] = values.astype(BF).reshape(NY, HD, LAT)
        omine[:, j, :, LAT:] = three_parts(level, side).reshape(NY, HD, QW - LAT)
        for d in range(1, NY):
            start(omine.at[lax.rem(y + d, NY), j], oin.at[d - 1, j], o_r[j], yp(d))

    for load in loads[1:]:
        load.wait()
    gate = jnp.zeros((SLOTS, FF), F32)
    up = jnp.zeros((SLOTS, FF), F32)
    for g in range(NE):
        gate = gate + jnp.dot(xn[g], wg[g * FEAT:(g + 1) * FEAT, :], preferred_element_type=F32)
        up = up + jnp.dot(xn[g], wu[g * FEAT:(g + 1) * FEAT, :], preferred_element_type=F32)
    hidden = (jax.nn.silu(gate) * up).astype(BF)

    def project(target):
        columns = pl.ds(pl.multiple_of(target * FEAT, BLK), FEAT)
        return jnp.dot(hidden, wd[:, columns], preferred_element_type=F32)

    yk = []
    for d in range(NY):
        ysib[d] = project(lax.rem(y + d + 1, NY) * 2 + 1 - k).astype(BF)
        yk.append(start(ysib.at[d], ysr.at[d], yk_r[d], sib))
    for d in range(NY):
        yown[d] = project(lax.rem(y + d + 1, NY) * 2 + k)
    for d in range(NY - 1):
        yk[d].wait_recv()
        ysend[d] = (yown[d] + ysr[d].astype(F32)).astype(BF)
    for h, (low, width) in enumerate(HALVES):
        for d in range(NY - 1):
            columns = pl.ds(low, width)
            start(ysend.at[d, :, columns], yrecv.at[d, :, columns], yy_r[h], yp(d + 1))

    back = Gather(og, start, back_r, x, z, e)
    for j in range(REQ):
        arrived(o_r[j], oin.at[:, j])
        values, level = merge([omine[y, j]] + [oin[d, j] for d in range(NY - 1)])
        og[z, j] = values.astype(BF)
        if j % 2 == 1:
            back.start((j - 1,))

    yk[NY - 1].wait_recv()
    first_rows = (((0,), (0,)), ((), ()))
    back.forward()
    for h, (low, width) in enumerate(HALVES):
        columns = pl.ds(low, width)
        arrived(yy_r[h], yrecv.at[:, :, columns])
        summed = yown[NY - 1, :, low:low + width] + ysr[NY - 1, :, low:low + width].astype(F32)
        for d in range(NY - 1):
            summed = summed + yrecv[d, :, low:low + width].astype(F32)
        rounded = summed.astype(BF)
        both = lax.dot_general(phi[...], rounded, first_rows, preferred_element_type=F32)
        both = both + lax.dot_general(plo[...], rounded, first_rows, preferred_element_type=F32)
        tw[:, :, low:low + width] = both.reshape(NX, 32, width)
        for d in range(1, NX):
            xrs[d - 1, :, low:low + width] = tw[lax.rem(x + d, NX), :, low:low + width].astype(BF)
            start(xrs.at[d - 1, :, columns], xrr.at[d - 1, :, columns], xr_r[h], xp(d))
    for h, (low, width) in enumerate(HALVES):
        arrived(xr_r[h], xrr.at[:, :, pl.ds(low, width)])
        own = tw[x, :, low:low + width]
        for d in range(NX - 1):
            own = own + xrr[d, :, low:low + width].astype(F32)
        for t in range(NZ):
            zs[h, t, 0:4, :] = own[4 * t:4 * t + 4, 0:256]
            zs[h, t, 4:8, 0:width - 256] = own[4 * t:4 * t + 4, 256:width]
            if width < 512:
                zs[h, t, 4:8, width - 256:256] = jnp.zeros((4, 512 - width), F32)
        for d in around:
            start(zs.at[h, lax.rem(z + d, NZ)], zr.at[h, d - 1], zr_r[h], zp(d))

    back.finish()
    for d in range(1, NX):
        target = lax.rem(x + d, NX)
        for j in range(REQ):
            r = table[2, (target * NZ + z) * REQ + j]
            oxs[d - 1, j] = og[bits(r, 2, NZ), bits(r, 0, REQ)]
        start(oxs.at[d - 1], oxr.at[x], ox_r, xp(d))
    for j in range(REQ):
        r = table[2, c * REQ + j]
        oxr[x, j] = og[bits(r, 2, NZ), bits(r, 0, REQ)]

    for h, (low, width) in enumerate(HALVES):
        arrived(zr_r[h], zr.at[h])
        final = zs[h, z]
        for d in range(NZ - 1):
            final = final + zr[h, d]
        moe_ref[:, low:low + 256] = final[0:4, :].astype(BF)
        moe_ref[:, low + 256:low + width] = final[4:8, 0:width - 256].astype(BF)
    moe_out = pltpu.make_async_copy(moe_ref, moe_hbm, out_sem.at[0])
    moe_out.start()
    att_out = pltpu.make_async_copy(att_ref, att_hbm, out_sem.at[1])

    arrived(ox_r, oxr.at[pl.ds(0, NX - 1)])
    for j in range(REQ):
        values = oxr[bits(table[2, c * REQ + j], 5, NX), j].astype(F32)
        for h in range(HD):
            af[j:j + 1, h * LAT:(h + 1) * LAT] = values[h:h + 1, :]
    att_ref[...] = af[...].astype(BF)
    att_out.start()
    for copy in pending[-SENDS:]:
        copy.wait_send()
    moe_out.wait()
    att_out.wait()


def layer(owner, lengths, routes, combine, q, qr, tok, gain, rope, lat, wg, wu, wd):
    hbm = pl.BlockSpec(memory_space=pltpu.HBM)
    dma = pltpu.SemaphoreType.DMA
    V = pltpu.VMEM
    return pl.pallas_call(
        layer_kernel,
        out_shape=(
            jax.ShapeDtypeStruct((REQ, HD * LAT), BF),
            jax.ShapeDtypeStruct((REQ, FEAT), BF),
        ),
        in_specs=[hbm] * 13,
        out_specs=(hbm, hbm),
        scratch_shapes=[
            V((REQ, HD * LAT), F32), V((REQ, HD * LAT), BF), V((REQ, FEAT), BF),
            pltpu.SMEM((1, REQ), jnp.int32), pltpu.SMEM((1, REQ), jnp.int32),
            pltpu.SMEM((REQ, 8), jnp.int32), pltpu.SMEM((REQ, 8), F32),
            V((REQ, HD * ROPE), BF), V((REQ, FEAT), BF), V((7, 128), F32), V((REQ, POS * ROPE), BF), V((REQ, POS // 2, 128), F32),
            pltpu.SMEM((8, 128), jnp.int32),
            V((D, FF), BF), V((D, FF), BF), V((FF, D), BF),
            V((REQ, POS, LAT), BF), V((REQ, POS, QW), BF),
            V((NZ, REQ, HD, QW), BF),
            V((NX, HD, QW), BF), V((NX, HD, QW), BF), V((NX, HD, QW), BF), V((NX, HD, QW), BF),
            V((NX - 1, REQ, HD, QW), BF),
            V((REQ, NE, HD, QW), BF),
            V((SLOTS, FEAT), BF), V((NE, SLOTS, FEAT), BF), V((NE, SLOTS, FEAT), BF),
            V((2, REQ, NY, HD, QW), BF), V((REQ, NY, HD, QW), BF),
            V((NY, REQ, HD, QW), BF), V((NY - 1, REQ, HD, QW), BF),
            V((NY, SLOTS, FEAT), BF), V((NY, SLOTS, FEAT), BF), V((NY, SLOTS, FEAT), F32),
            V((NY - 1, SLOTS, FEAT), BF), V((NY - 1, SLOTS, FEAT), BF),
            V((NX, 32, FEAT), F32),
            V((NX - 1, 32, FEAT), BF), V((NX - 1, 32, FEAT), BF),
            V((2, NZ, 8, 256), F32), V((2, NZ - 1, 8, 256), F32),
            V((NZ, REQ, HD, LAT), BF),
            V((NX - 1, REQ, HD, LAT), BF), V((NX, REQ, HD, LAT), BF),
            V((16, 256), F32), V((16, 256), BF), V((NX, NZ, 16, 256), BF),
            V((NE, 7, 128), F32),
            V((NZ, 8, 128), F32), V((NZ, 8, 128), F32),
            V((8, 128), F32), V((NX, 8, 128), F32), V((8, 128), F32),
            V((NZ, 8, 128), jnp.int32), V((NX, 8, 128), jnp.int32), V((8, 128), jnp.int32),
            V((SLOTS, 128), BF), V((SLOTS, 128), BF),
            dma((4,)), dma((9,)), dma((1,)), dma((2,)), dma((SENDS,)), dma((RECVS,)),
        ],
        compiler_params=pltpu.CompilerParams(
            collective_id=0, has_side_effects=True, vmem_limit_bytes=64 * 1024 * 1024
        ),
    )(owner, lengths, routes, combine, q, qr, tok, gain, rope, lat, wg, wu, wd)


def hand_on_kernel(a_ref, b_ref, c_ref, d_ref):
    c_ref[...] = a_ref[...]
    d_ref[...] = b_ref[...]


def hand_on(a, b):
    hbm = pl.BlockSpec(memory_space=pltpu.VMEM)
    return pl.pallas_call(
        hand_on_kernel,
        out_shape=(jax.ShapeDtypeStruct(a.shape, a.dtype), jax.ShapeDtypeStruct(b.shape, b.dtype)),
        in_specs=[hbm, hbm],
        out_specs=(hbm, hbm),
        compiler_params=pltpu.CompilerParams(vmem_limit_bytes=64 * 1024 * 1024),
    )(a, b)


def local(
    latent_plane,
    latent_rope,
    query_plane,
    query_rope,
    decode_hidden,
    lengths,
    owner,
    norm_gain,
    routes,
    combine,
    gate_weight,
    up_weight,
    down_weight,
):
    attended, summed = layer(
        owner, lengths, routes, combine, query_plane, query_rope, decode_hidden,
        norm_gain.reshape(7, 128), latent_rope, latent_plane, gate_weight, up_weight, down_weight,
    )
    return hand_on(attended, summed)


def solution(mesh):
    placed = (
        P("ctx", "expert", None),
        P("ctx", "expert"),
        P("ctx", "expert", None),
        P("ctx", "expert"),
        P("ctx", "expert"),
        P("ctx", None),
        P("ctx", None),
        P("expert"),
        P("ctx", None),
        P("ctx", None),
        P("ctx", None, "expert"),
        P("ctx", None, "expert"),
        P("ctx", "expert", None),
    )
    return jax.shard_map(
        local,
        mesh=mesh,
        in_specs=placed,
        out_specs=(P("ctx", "expert"), P("ctx", "expert")),
        check_vma=False,
    )
```

```python
import functools

import jax
import jax.numpy as jnp
from jax import lax
from jax.experimental import pallas as pl
from jax.experimental.pallas import tpu as pltpu
from jax.sharding import PartitionSpec as P

D = 7168
LAT = 512
ROPE = 64
BLK = 128
NX = 4
NZ = 8
NE = 8
NY = 4
REQ = 4
HD = 16
QW = 640
POS = 256
CAP = 3
SLOTS = NX * NZ * CAP
SENDS = 48
RECVS = 72
HALVES = ((0, 512), (512, 384))
FEAT = D // NE
FF = 256

MESH = pl.DeviceIdType.MESH
BF = jnp.bfloat16
F32 = jnp.float32
score_scale = 192.0 ** (-0.5)
pack_limit = 448.0
HIDDEN_SCORE = -1e30


def coordinates():
    c = lax.axis_index("ctx")
    e = lax.axis_index("expert")
    return c, e, lax.div(c, NZ), lax.rem(c, NZ), lax.div(e, 2), lax.rem(e, 2)


def greet(peers):
    barrier = pltpu.get_barrier_semaphore()
    for peer in peers:
        pl.semaphore_signal(barrier, inc=1, device_id=peer, device_id_type=MESH)
    return lambda: pl.semaphore_wait(barrier, len(peers))


def remote(src, dst, send_sem, recv_sem, peer):
    return pltpu.make_async_remote_copy(
        src_ref=src,
        dst_ref=dst,
        send_sem=send_sem,
        recv_sem=recv_sem,
        device_id=peer,
        device_id_type=MESH,
    )


class Gather:
    def __init__(self, buf, start, sems, x, z, e):
        self.buf, self.start_copy, self.sems = buf, start, sems
        self.x, self.z, self.e = x, z, e
        self.second = {}

    def put(self, origin, hop, sign, low):
        block = self.buf.at[lax.rem(self.z + 2 * NZ - sign * origin, NZ), pl.ds(low, 2)]
        peer = (self.x * NZ + lax.rem(self.z + 2 * NZ + sign * hop, NZ), self.e)
        if origin + hop == 2:
            sem = self.sems[len(self.second)]
            self.second[sign, low] = self.start_copy(block, block, sem, peer)
        else:
            self.start_copy(block, block, self.sems[4], peer)

    def start(self, lows=(0, 2)):
        for hop in (2, 1):
            for low in lows:
                for sign in (1, -1):
                    self.put(0, hop, sign, low)

    def forward(self):
        for first in (True, False):
            for sign in (1, -1):
                low = 0 if first == (sign == 1) else 2
                self.second[sign, low].wait_recv()
                if first:
                    self.put(2, 2, sign, low)
                self.put(2, 1, sign, low)

    def finish(self):
        arrived(self.sems[4], self.buf.at[pl.ds(0, 5)])


def arrived(sem, blocks):
    pltpu.make_async_copy(blocks, blocks, sem).wait()


def three_parts(level, side):
    first = level.astype(BF).astype(F32)
    second = (level - first).astype(BF).astype(F32)
    third = level - first - second
    return jnp.where(side == 0, first, jnp.where(side == 1, second, jnp.where(side == 2, third, 0.0))).astype(BF)


def merge(parts):
    levels = [jnp.sum(part[:, LAT:].astype(F32), axis=-1, keepdims=True) for part in parts]
    top = functools.reduce(jnp.maximum, levels)
    share = [jnp.exp(level - top) for level in levels]
    total = functools.reduce(jnp.add, share)
    acc = share[0] * parts[0][:, :LAT].astype(F32)
    for weight, part in zip(share[1:], parts[1:]):
        acc = acc + weight * part[:, :LAT].astype(F32)
    return acc / total, top + jnp.log(total)


def bits(number, shift, count):
    return jnp.bitwise_and(jnp.right_shift(number, shift), count - 1)


def iota(shape, axis):
    return lax.broadcasted_iota(jnp.int32, shape, axis)


def layer_kernel(
    owner_hbm, length_hbm, routes_hbm, combine_hbm,
    q_hbm, qr_hbm, tok_hbm, gain_hbm, rope_hbm,
    lat_hbm, wg_hbm, wu_hbm, wd_hbm,
    att_hbm, moe_hbm,
    af, att_ref, moe_ref, owner_ref, length_ref, routes_ref, combine_ref, qr_ref, tok_ref, gain_ref, rope_ref, ropef, table, wg, wu, wd, lat, kcat, qz, xbuf0, xbuf1, xbuf2, xbuf3, xsend, qall, xt, tall, xn, opart, osib, omine, oin,
    ysib, ysr, yown, ysend, yrecv, tw, xrs, xrr, zs, zr, og, oxs, oxr0, oxr1, oxr2, oxr3,
    tokf, tokb, tk, gall, mzs, mzr, mxs, mxr, mrow, owz, owx, tbl, phi, plo,
    w_sem, s_sem, t_sem, out_sem, send_sems, recv_sems,
):
    c, e, x, z, y, k = coordinates()
    pending = []
    oxr = (oxr0, oxr1, oxr2, oxr3)
    xbuf = (xbuf0, xbuf1, xbuf2, xbuf3)

    def zp(d):
        return (x * NZ + lax.rem(z + d, NZ), e)

    def xp(d):
        return (lax.rem(x + d, NX) * NZ + z, e)

    def ep(d):
        return (c, lax.rem(e + d, NE))

    def yp(d):
        return (c, lax.rem(y + d, NY) * 2 + k)

    sib = (c, y * 2 + 1 - k)

    def start(src, dst, recv_sem, peer):
        n = len(pending)
        if n >= SENDS:
            pending[n - SENDS].wait_send()
        copy = remote(src, dst, send_sems.at[n % SENDS], recv_sem, peer)
        copy.start()
        pending.append(copy)
        return copy

    taken = [0]

    def take(count):
        taken[0] += count
        return [recv_sems.at[taken[0] - count + n] for n in range(count)]

    oz_r, mz_r, kz_r, wx_r, mx_r, kx_r, g_r, tk_r = take(8)
    yy_r, xr_r, zr_r = take(2), take(2), take(2)
    qx_r, qk_r, os_r, o_r, yk_r, ox_r = (take(4) for _ in range(6))
    ty_r, qy_r, gather_r, back_r = take(12), take(12), take(5), take(5)

    loads = [
        pltpu.make_async_copy(lat_hbm, lat, w_sem.at[0]),
        pltpu.make_async_copy(wg_hbm.at[0], wg, w_sem.at[1]),
        pltpu.make_async_copy(wu_hbm.at[0], wu, w_sem.at[2]),
        pltpu.make_async_copy(wd_hbm.at[0], wd, w_sem.at[3]),
    ]
    blocks = (
        (routes_hbm, routes_ref), (combine_hbm, combine_ref), (owner_hbm, owner_ref), (length_hbm, length_ref),
        (qr_hbm, qr_ref), (q_hbm, qz.at[z, :, :, pl.ds(0, LAT)]), (tok_hbm, tok_ref), (gain_hbm, gain_ref),
        (rope_hbm, rope_ref),
    )
    small = [pltpu.make_async_copy(src, dst, s_sem.at[n]) for n, (src, dst) in enumerate(blocks)]
    for load in small:
        load.start()
    loads[0].start()
    wait_for_all = greet(
        [zp(d) for d in range(1, NZ)] + [xp(d) for d in range(1, NX)] + [ep(d) for d in range(1, NE)]
    )
    for load in loads[1:]:
        load.start()
    for load in small[:-1]:
        load.wait()

    lane = iota((1, 128), 1)
    mine = jnp.zeros((1, 128), jnp.int32)
    for j in range(REQ):
        mine = jnp.where(lane == c * REQ + j, owner_ref[0, j], mine)
    owz[z] = mine
    row = iota((32, 128), 0)
    expert = jnp.bitwise_and(row, 3) * NZ + jnp.right_shift(row, 2)
    wide = iota((32, 128), 1)
    weights = jnp.zeros((32, 128), F32)
    for j in range(REQ):
        for n in range(8):
            hit = (expert == routes_ref[j, n]) & (wide == c * REQ + j)
            weights = jnp.where(hit, combine_ref[j, n], weights)
    mzs[...] = weights.reshape(NZ, NX, 128)
    state = tok_ref[...].astype(F32)
    for g in range(4):
        width = 256 if g < 3 else 128
        tokf[4 * g:4 * g + 4, 0:width] = state[:, g * 256:g * 256 + width]
    tokf[12:16, 128:256] = jnp.zeros((4, 128), F32)
    tokb[...] = tokf[...].astype(BF)
    gall[e] = gain_ref[...]
    turned = jnp.concatenate(
        [
            jnp.where(
                jnp.right_shift(iota((HD, HD * ROPE), 1), 6) == iota((HD, HD * ROPE), 0),
                jnp.broadcast_to(qr_ref[...].astype(F32)[j:j + 1, :], (HD, HD * ROPE)),
                0.0,
            )
            for j in range(REQ)
        ],
        axis=0,
    ).astype(BF)
    fold = (jnp.bitwise_and(iota((HD * ROPE, 128), 0), 63) == iota((HD * ROPE, 128), 1)).astype(F32).astype(BF)
    qz[z, :, :, LAT:] = jnp.dot(turned, fold, preferred_element_type=F32).astype(BF).reshape(REQ, HD, 128)

    wait_for_all()
    around = (1, 7, 2, 6, 3, 5, 4)
    for d in around:
        start(owz.at[z], owz.at[z], oz_r, zp(d))
    for d in around:
        start(mzs.at[lax.rem(z + d, NZ)], mzr.at[z], mz_r, zp(d))
    for d in around:
        start(tokb, tk.at[x, z], kz_r, zp(d))
    gather = Gather(qz, start, gather_r, x, z, e)
    gather.start()
    for d in range(1, NE):
        start(gain_ref, gall.at[e], g_r, ep(d))
    mzr[z] = mzs[z]
    tk[x, z] = tokb[...]

    small[-1].wait()
    for t in range(POS // 2):
        ropef[:, t, :] = rope_ref[:, t * 128:(t + 1) * 128].astype(F32)
    position = iota((POS, POS // 2), 0)
    pair = iota((POS, POS // 2), 1) * 2
    even = (position == pair).astype(F32).astype(BF)
    odd = (position == pair + 1).astype(F32).astype(BF)
    low = iota((POS // 2, 128), 1) < ROPE
    for j in range(REQ):
        rows = ropef[j]
        near = jnp.where(low, rows, 0.0).astype(BF)
        far = jnp.where(low, pltpu.roll(rows, ROPE, 1), 0.0).astype(BF)
        turned = jnp.dot(even, near, preferred_element_type=F32) + jnp.dot(odd, far, preferred_element_type=F32)
        kcat[j, :, LAT:] = turned.astype(BF)

    loads[0].wait()
    for j in range(REQ):
        for b in range(LAT // BLK):
            block = lat[j, :, b * BLK:(b + 1) * BLK].astype(F32)
            scale = ((jnp.max(jnp.abs(block), axis=-1, keepdims=True) + 1e-06) / pack_limit).astype(BF)
            scale = scale.astype(F32)
            packed = (block / scale).astype(BF)
            kcat[j, :, b * BLK:(b + 1) * BLK] = (packed.astype(F32) * scale).astype(BF)

    arrived(oz_r, owz.at[pl.ds(0, NZ - 1)])
    arrived(mz_r, mzr.at[pl.ds(0, NZ - 1)])
    owx[x] = functools.reduce(jnp.add, [owz[d] for d in range(NZ)])
    mxs[...] = functools.reduce(jnp.add, [mzr[d] for d in range(NZ)])
    mxr[x] = mxs[...]
    for d in range(1, NX):
        start(owx.at[x], owx.at[x], wx_r, xp(d))
    for d in range(1, NX):
        start(mxs, mxr.at[x], mx_r, xp(d))
    arrived(kz_r, tk.at[0, pl.ds(0, NZ - 1)])
    for d in range(1, NX):
        start(tk.at[x], tk.at[x], kx_r, xp(d))
    gather.forward()

    arrived(wx_r, owx.at[pl.ds(0, NX - 1)])
    arrived(mx_r, mxr.at[pl.ds(0, NX - 1)])
    sub = iota((128, 128), 0)
    col = iota((128, 128), 1)
    owners = functools.reduce(jnp.add, [owx[d] for d in range(NX)])
    across = jnp.broadcast_to(owners, (128, 128))
    rank = jnp.sum(jnp.where((across.T == across) & (sub < col), 1, 0), axis=0, keepdims=True)
    place = jnp.broadcast_to(owners * REQ + rank, (128, 128)).T
    request_of = jnp.sum(jnp.where(place == col, sub, 0), axis=0, keepdims=True)
    eight = iota((8, 128), 0)
    tbl[...] = jnp.where(eight == 0, owners, jnp.where(eight == 1, rank, request_of))
    to_scalars = pltpu.make_async_copy(tbl, table, t_sem.at[0])
    to_scalars.start()

    mrow[...] = functools.reduce(jnp.add, [mxr[d] for d in range(NX)])
    share = mrow[pl.ds(x, 1), :]
    chosen = jnp.where(share > 0, 1.0, 0.0)
    earlier = ((jnp.right_shift(sub, 2) == jnp.right_shift(col, 2)) & (sub < col)).astype(F32).astype(BF)
    before = jnp.dot(jnp.broadcast_to(chosen, (8, 128)).astype(BF), earlier, preferred_element_type=F32)[0:1, :]
    slot = (jnp.right_shift(iota((1, 128), 1), 2) * CAP).astype(F32) + before
    placing = jnp.where(iota((SLOTS, 128), 0).astype(F32) == slot, chosen, 0.0)
    scaled = placing * share
    high = scaled.astype(BF)
    phi[...] = high
    plo[...] = (scaled - high.astype(F32)).astype(BF)
    token_of = iota((128, 512), 1)
    token_of = jnp.right_shift(token_of, 4) * REQ + jnp.bitwise_and(token_of, 3)
    widen = (token_of == iota((128, 512), 0)).astype(F32).astype(BF)
    placing = jnp.dot(placing.astype(BF), widen, preferred_element_type=F32)
    group = jnp.bitwise_and(jnp.right_shift(iota((SLOTS, 512), 1), 2), 3)
    arrived(kx_r, tk.at[pl.ds(0, NX - 1)])
    states = tk[...].reshape(512, 256)
    ty = []
    for g in range(4):
        width = 256 if g < 3 else 128
        part = jnp.where(group == g, placing, 0.0).astype(BF)
        columns = pl.ds(g * 256, width)
        xt[:, g * 256:g * 256 + width] = jnp.dot(
            part, states[:, 0:width], preferred_element_type=F32
        ).astype(BF)
        for d in range(1, NY):
            ty.append(start(xt.at[:, columns], tall.at[e, :, columns], ty_r[g * 3 + d - 1], yp(d)))
        start(xt.at[:, columns], tall.at[e, :, columns], tk_r, sib)

    tall[e] = xt[...]

    gather.finish()
    to_scalars.wait()
    for j in range(REQ):
        for d in range(1, NX):
            r = (lax.rem(x + d, NX) * NZ + z) * REQ + j
            xsend[d - 1, j] = qz[bits(table[0, r], 0, NZ), bits(table[1, r], 0, REQ)]
            start(xsend.at[d - 1, j], xbuf[j].at[x], qx_r[j], xp(d))
        r = c * REQ + j
        xbuf[j][x] = qz[bits(table[0, r], 0, NZ), bits(table[1, r], 0, REQ)]

    qy = []
    for j in range(REQ):
        arrived(qx_r[j], xbuf[j].at[pl.ds(0, NX - 1)])
        qall[j, e] = xbuf[j][bits(table[0, c * REQ + j], 3, NX)]
        block = qall.at[j, e]
        for d in range(1, NY):
            qy.append(start(block, block, qy_r[j * 3 + d - 1], yp(d)))
        start(block, block, qk_r[j], sib)
    for g in range(4):
        for d in range(1, NY):
            ty[g * 3 + d - 1].wait_recv()
            other = lax.rem(y + NY - d, NY) * 2 + k
            block = tall.at[other, :, pl.ds(g * 256, 256 if g < 3 else 128)]
            start(block, block, tk_r, sib)
    for j in range(REQ):
        for d in range(1, NY):
            qy[j * 3 + d - 1].wait_recv()
            block = qall.at[j, lax.rem(y + NY - d, NY) * 2 + k]
            start(block, block, qk_r[j], sib)

    lanes = iota((1, POS), 1) + e * POS
    side = iota((HD * NE, QW - LAT), 1)
    oc = []
    for j in range(REQ):
        arrived(qk_r[j], qall.at[j, pl.ds(0, NY)])
        scores = lax.dot_general(
            qall[j].reshape(NE * HD, QW), kcat[j], (((1,), (1,)), ((), ())), preferred_element_type=F32
        )
        scores = jnp.where(lanes < length_ref[0, j], scores * score_scale, HIDDEN_SCORE)
        highest = jnp.max(scores, axis=-1, keepdims=True)
        likely = jnp.exp(scores - highest)
        total = jnp.sum(likely, axis=-1, keepdims=True)
        out = jnp.dot(likely.astype(BF), kcat[j, :, :LAT], preferred_element_type=F32) / total
        tail = three_parts(highest + jnp.log(total), side)
        out = out.astype(BF).reshape(NY, 2, HD, LAT)
        tail = tail.reshape(NY, 2, HD, QW - LAT)
        for core in range(2):
            opart[core, j, :, :, :LAT] = out[:, core]
            opart[core, j, :, :, LAT:] = tail[:, core]
        oc.append(start(opart.at[1 - k, j], osib.at[j], os_r[j], sib))

    arrived(tk_r, tall.at[pl.ds(0, NY)])
    arrived(g_r, gall.at[pl.ds(0, NE - 1)])
    squares = jnp.zeros((SLOTS, 1), F32)
    for g in range(NE):
        rows = tall[g].astype(F32)
        squares = squares + jnp.sum(rows * rows, axis=-1, keepdims=True)
    inverse = lax.rsqrt(squares / D + 1e-06)
    for g in range(NE):
        for b in range(FEAT // 128):
            part = tall[g, :, b * 128:(b + 1) * 128].astype(F32)
            xn[g, :, b * 128:(b + 1) * 128] = (part * inverse * gall[g, b:b + 1, :]).astype(BF)

    side = iota((NY * HD, QW - LAT), 1)
    for j in range(REQ):
        oc[j].wait_recv()
        values, level = merge([opart[k, j].reshape(NY * HD, QW), osib[j].reshape(NY * HD, QW)])
        omine[:, j, :, :LAT] = values.astype(BF).reshape(NY, HD, LAT)
        omine[:, j, :, LAT:] = three_parts(level, side).reshape(NY, HD, QW - LAT)
        for d in range(1, NY):
            start(omine.at[lax.rem(y + d, NY), j], oin.at[d - 1, j], o_r[j], yp(d))

    for load in loads[1:]:
        load.wait()
    gate = jnp.zeros((SLOTS, FF), F32)
    up = jnp.zeros((SLOTS, FF), F32)
    for g in range(NE):
        gate = gate + jnp.dot(xn[g], wg[g * FEAT:(g + 1) * FEAT, :], preferred_element_type=F32)
        up = up + jnp.dot(xn[g], wu[g * FEAT:(g + 1) * FEAT, :], preferred_element_type=F32)
    hidden = (jax.nn.silu(gate) * up).astype(BF)

    def project(target):
        columns = pl.ds(pl.multiple_of(target * FEAT, BLK), FEAT)
        return jnp.dot(hidden, wd[:, columns], preferred_element_type=F32)

    yk = []
    for d in range(NY):
        ysib[d] = project(lax.rem(y + d + 1, NY) * 2 + 1 - k).astype(BF)
        yk.append(start(ysib.at[d], ysr.at[d], yk_r[d], sib))
    for d in range(NY):
        yown[d] = project(lax.rem(y + d + 1, NY) * 2 + k)
    for d in range(NY - 1):
        yk[d].wait_recv()
        ysend[d] = (yown[d] + ysr[d].astype(F32)).astype(BF)
    for h, (low, width) in enumerate(HALVES):
        for d in range(NY - 1):
            columns = pl.ds(low, width)
            start(ysend.at[d, :, columns], yrecv.at[d, :, columns], yy_r[h], yp(d + 1))

    back = Gather(og, start, back_r, x, z, e)
    for j in range(REQ):
        arrived(o_r[j], oin.at[:, j])
        values, level = merge([omine[y, j]] + [oin[d, j] for d in range(NY - 1)])
        og[z, j] = values.astype(BF)
        if j % 2 == 1:
            back.start((j - 1,))

    yk[NY - 1].wait_recv()
    first_rows = (((0,), (0,)), ((), ()))
    back.forward()
    for h, (low, width) in enumerate(HALVES):
        columns = pl.ds(low, width)
        arrived(yy_r[h], yrecv.at[:, :, columns])
        summed = yown[NY - 1, :, low:low + width] + ysr[NY - 1, :, low:low + width].astype(F32)
        for d in range(NY - 1):
            summed = summed + yrecv[d, :, low:low + width].astype(F32)
        rounded = summed.astype(BF)
        both = lax.dot_general(phi[...], rounded, first_rows, preferred_element_type=F32)
        both = both + lax.dot_general(plo[...], rounded, first_rows, preferred_element_type=F32)
        tw[:, :, low:low + width] = both.reshape(NX, 32, width)
        for d in range(1, NX):
            xrs[d - 1, :, low:low + width] = tw[lax.rem(x + d, NX), :, low:low + width].astype(BF)
            start(xrs.at[d - 1, :, columns], xrr.at[d - 1, :, columns], xr_r[h], xp(d))
    for h, (low, width) in enumerate(HALVES):
        arrived(xr_r[h], xrr.at[:, :, pl.ds(low, width)])
        own = tw[x, :, low:low + width]
        for d in range(NX - 1):
            own = own + xrr[d, :, low:low + width].astype(F32)
        for t in range(NZ):
            zs[h, t, 0:4, :] = own[4 * t:4 * t + 4, 0:256]
            zs[h, t, 4:8, 0:width - 256] = own[4 * t:4 * t + 4, 256:width]
            if width < 512:
                zs[h, t, 4:8, width - 256:256] = jnp.zeros((4, 512 - width), F32)
        for d in around:
            start(zs.at[h, lax.rem(z + d, NZ)], zr.at[h, d - 1], zr_r[h], zp(d))

    back.finish()
    for j in range(REQ):
        for d in range(1, NX):
            r = table[2, (lax.rem(x + d, NX) * NZ + z) * REQ + j]
            oxs[d - 1, j] = og[bits(r, 2, NZ), bits(r, 0, REQ)]
            start(oxs.at[d - 1, j], oxr[j].at[x], ox_r[j], xp(d))
        r = table[2, c * REQ + j]
        oxr[j][x] = og[bits(r, 2, NZ), bits(r, 0, REQ)]

    for h, (low, width) in enumerate(HALVES):
        arrived(zr_r[h], zr.at[h])
        final = zs[h, z]
        for d in range(NZ - 1):
            final = final + zr[h, d]
        moe_ref[:, low:low + 256] = final[0:4, :].astype(BF)
        moe_ref[:, low + 256:low + width] = final[4:8, 0:width - 256].astype(BF)
    moe_out = pltpu.make_async_copy(moe_ref, moe_hbm, out_sem.at[0])
    moe_out.start()
    att_out = pltpu.make_async_copy(att_ref, att_hbm, out_sem.at[1])

    for j in range(REQ):
        arrived(ox_r[j], oxr[j].at[pl.ds(0, NX - 1)])
        values = oxr[j][bits(table[2, c * REQ + j], 5, NX)].astype(F32)
        for h in range(HD):
            af[j:j + 1, h * LAT:(h + 1) * LAT] = values[h:h + 1, :]
    att_ref[...] = af[...].astype(BF)
    att_out.start()
    for copy in pending[-SENDS:]:
        copy.wait_send()
    moe_out.wait()
    att_out.wait()


def layer(owner, lengths, routes, combine, q, qr, tok, gain, rope, lat, wg, wu, wd):
    hbm = pl.BlockSpec(memory_space=pltpu.HBM)
    dma = pltpu.SemaphoreType.DMA
    V = pltpu.VMEM
    return pl.pallas_call(
        layer_kernel,
        out_shape=(
            jax.ShapeDtypeStruct((REQ, HD * LAT), BF),
            jax.ShapeDtypeStruct((REQ, FEAT), BF),
        ),
        in_specs=[hbm] * 13,
        out_specs=(hbm, hbm),
        scratch_shapes=[
            V((REQ, HD * LAT), F32), V((REQ, HD * LAT), BF), V((REQ, FEAT), BF),
            pltpu.SMEM((1, REQ), jnp.int32), pltpu.SMEM((1, REQ), jnp.int32),
            pltpu.SMEM((REQ, 8), jnp.int32), pltpu.SMEM((REQ, 8), F32),
            V((REQ, HD * ROPE), BF), V((REQ, FEAT), BF), V((7, 128), F32), V((REQ, POS * ROPE), BF), V((REQ, POS // 2, 128), F32),
            pltpu.SMEM((8, 128), jnp.int32),
            V((D, FF), BF), V((D, FF), BF), V((FF, D), BF),
            V((REQ, POS, LAT), BF), V((REQ, POS, QW), BF),
            V((NZ, REQ, HD, QW), BF),
            V((NX, HD, QW), BF), V((NX, HD, QW), BF), V((NX, HD, QW), BF), V((NX, HD, QW), BF),
            V((NX - 1, REQ, HD, QW), BF),
            V((REQ, NE, HD, QW), BF),
            V((SLOTS, FEAT), BF), V((NE, SLOTS, FEAT), BF), V((NE, SLOTS, FEAT), BF),
            V((2, REQ, NY, HD, QW), BF), V((REQ, NY, HD, QW), BF),
            V((NY, REQ, HD, QW), BF), V((NY - 1, REQ, HD, QW), BF),
            V((NY, SLOTS, FEAT), BF), V((NY, SLOTS, FEAT), BF), V((NY, SLOTS, FEAT), F32),
            V((NY - 1, SLOTS, FEAT), BF), V((NY - 1, SLOTS, FEAT), BF),
            V((NX, 32, FEAT), F32),
            V((NX - 1, 32, FEAT), BF), V((NX - 1, 32, FEAT), BF),
            V((2, NZ, 8, 256), F32), V((2, NZ - 1, 8, 256), F32),
            V((NZ, REQ, HD, LAT), BF),
            V((NX - 1, REQ, HD, LAT), BF), V((NX, HD, LAT), BF), V((NX, HD, LAT), BF), V((NX, HD, LAT), BF), V((NX, HD, LAT), BF),
            V((16, 256), F32), V((16, 256), BF), V((NX, NZ, 16, 256), BF),
            V((NE, 7, 128), F32),
            V((NZ, NX, 128), F32), V((NZ, NX, 128), F32),
            V((NX, 128), F32), V((NX, NX, 128), F32), V((NX, 128), F32),
            V((NZ, 1, 128), jnp.int32), V((NX, 1, 128), jnp.int32), V((8, 128), jnp.int32),
            V((SLOTS, 128), BF), V((SLOTS, 128), BF),
            dma((4,)), dma((9,)), dma((1,)), dma((2,)), dma((SENDS,)), dma((RECVS,)),
        ],
        compiler_params=pltpu.CompilerParams(
            collective_id=0, has_side_effects=True, vmem_limit_bytes=64 * 1024 * 1024
        ),
    )(owner, lengths, routes, combine, q, qr, tok, gain, rope, lat, wg, wu, wd)


def hand_on_kernel(a_ref, b_ref, c_ref, d_ref):
    c_ref[...] = a_ref[...]
    d_ref[...] = b_ref[...]


def hand_on(a, b):
    hbm = pl.BlockSpec(memory_space=pltpu.VMEM)
    return pl.pallas_call(
        hand_on_kernel,
        out_shape=(jax.ShapeDtypeStruct(a.shape, a.dtype), jax.ShapeDtypeStruct(b.shape, b.dtype)),
        in_specs=[hbm, hbm],
        out_specs=(hbm, hbm),
        compiler_params=pltpu.CompilerParams(vmem_limit_bytes=64 * 1024 * 1024),
    )(a, b)


def local(
    latent_plane,
    latent_rope,
    query_plane,
    query_rope,
    decode_hidden,
    lengths,
    owner,
    norm_gain,
    routes,
    combine,
    gate_weight,
    up_weight,
    down_weight,
):
    attended, summed = layer(
        owner, lengths, routes, combine, query_plane, query_rope, decode_hidden,
        norm_gain.reshape(7, 128), latent_rope, latent_plane, gate_weight, up_weight, down_weight,
    )
    return hand_on(attended, summed)


def solution(mesh):
    placed = (
        P("ctx", "expert", None),
        P("ctx", "expert"),
        P("ctx", "expert", None),
        P("ctx", "expert"),
        P("ctx", "expert"),
        P("ctx", None),
        P("ctx", None),
        P("expert"),
        P("ctx", None),
        P("ctx", None),
        P("ctx", None, "expert"),
        P("ctx", None, "expert"),
        P("ctx", "expert", None),
    )
    return jax.shard_map(
        local,
        mesh=mesh,
        in_specs=placed,
        out_specs=(P("ctx", "expert"), P("ctx", "expert")),
        check_vma=False,
    )
```
